128 devices in a mesh: ctx: 32 (over y_lo, x, z), fsdp: 4 (over y_hi, core).
Axes of the slice: x: 4, y: 4 (y_hi: 2, y_lo: 2; y = y_hi * 2 + y_lo), z: 4, core: 2. Of those that a mesh axis runs over, the one named last changes fastest.
Arguments:
- query_rows: bfloat16 [16384, 4096], P('ctx', 'fsdp'), may hold values from -9 to 9
- key_rows: bfloat16 [16384, 4096], P('ctx', 'fsdp'), may hold values from -6 to 6
- value_rows: bfloat16 [16384, 4096], P('ctx', 'fsdp'), may hold values from -9 to 9
- gate_input: bfloat16 [16384, 4096], P('ctx', 'fsdp'), may hold values from -6 to 6
- norm_gain: float32 [4096], P('fsdp'), may hold values from 0.5 to 1.5
- w_out: bfloat16 [4096, 3072], P(None, 'fsdp'), may hold values from -0.09375 to 0.09375
- mixed_grad: bfloat16 [16384, 3072], P('ctx', 'fsdp'), may hold values from -6 to 6
Outputs:
- mixed: bfloat16 [16384, 3072], P('ctx', 'fsdp')
- w_out_grad: float32 [4096, 3072], P('ctx', 'fsdp')
- query_grad: bfloat16 [16384, 4096], P('ctx', 'fsdp')
- key_grad: bfloat16 [16384, 4096], P('ctx', 'fsdp')
- value_grad: bfloat16 [16384, 4096], P('ctx', 'fsdp')
- gate_grad: bfloat16 [16384, 4096], P('ctx', 'fsdp')
The draws below stay inside these ranges and needn't reach their ends.
All inputs are finite; a program needn't handle non-finite values.
Results may differ from the reference program's by a relative error of at most 0.005.
Values may be sent and summed in bfloat16 or wider, within the bound.
No kernel may reach another device: no remote copies, remote signals or barrier semaphores. Data moves between devices by JAX's collectives and lax.ppermute only.
A program may use at most 192 MiB of HBM per device.

```python
import math
import jax
import jax.numpy as jnp
from jax import lax

D = 3072
HEADS = 32
HD = 128
TOK_DEV = 512
INNER = 4096
TOKENS = 16384


def draw_query_rows(key, part):
    key = jax.random.fold_in(key, 17)
    base_key, scale_key = jax.random.split(key)
    base = jnp.clip(jax.random.normal(base_key, (TOKENS, HEADS * HD), jnp.float32), -4.0, 4.0)
    scales = jnp.exp(jax.random.uniform(scale_key, (TOKENS, 1), jnp.float32, math.log(0.5), math.log(2.0)))
    return (base * scales).astype(jnp.bfloat16)


def draw_value_rows(key, part):
    key = jax.random.fold_in(key, 29)
    base_key, scale_key = jax.random.split(key)
    base = jnp.clip(jax.random.normal(base_key, (TOKENS, HEADS * HD), jnp.float32), -4.0, 4.0)
    scales = jnp.exp(jax.random.uniform(scale_key, (1, HEADS * HD), jnp.float32, math.log(0.5), math.log(2.0)))
    return (base * scales).astype(jnp.bfloat16)


def shard_levels(stream_key, extent, pieces, least, largest):
    level, own = 1.0, jax.random.fold_in(stream_key, 6)
    for dim, parts in pieces:
        draws = jnp.exp(jax.random.uniform(jax.random.fold_in(own, dim), (parts,), jnp.float32, least / len(pieces), largest / len(pieces)))
        level = level * jnp.repeat(draws, extent[dim] // parts).reshape([-1 if axis == dim else 1 for axis in range(len(extent))])
    return level


def bell_draw(rng, shape, deviation, most, shards=(), dtype=jnp.bfloat16):
    loudness = shard_levels(rng, shape, shards, -0.22, 0.18) if shards else 1.0
    entries = jax.random.normal(rng, shape, jnp.float32) * deviation * loudness
    return jnp.minimum(jnp.maximum(entries, -most), most).astype(dtype)


def setup_inputs(seed: int = 0) -> dict:
    seeds = jax.random.split(jax.random.key(seed), 8)
    return {
        "query_rows": draw_query_rows(jax.random.fold_in(seeds[7], 71), 0),
        "key_rows": bell_draw(seeds[1], (TOKENS, INNER), 1.0, 6.0, ((0, 32), (1, 4))),
        "value_rows": draw_value_rows(jax.random.fold_in(seeds[7], 71), 0),
        "gate_input": bell_draw(seeds[3], (TOKENS, INNER), 1.5, 6.0, ((0, 32), (1, 4))),
        "norm_gain": jnp.clip(0.5 + 1.0 * jax.random.uniform(seeds[4], (INNER,), jnp.float32) ** shard_levels(seeds[4], (INNER,), ((0, 4),), -0.2, 0.2), 0.5, 1.5),
        "w_out": bell_draw(seeds[5], (INNER, D), INNER ** -0.5, 0.09375, ((1, 4),)),
        "mixed_grad": bell_draw(seeds[6], (TOKENS, D), 1.0, 6.0, ((0, 32), (1, 4))),
    }


highest = lax.Precision.HIGHEST

def causal_mask(length):
    row_index = lax.broadcasted_iota(jnp.int32, (length, length), 0)
    col_index = lax.broadcasted_iota(jnp.int32, (length, length), 1)
    return (col_index <= row_index).astype(jnp.float32)

def reference(query_rows, key_rows, value_rows, gate_input, norm_gain, w_out, mixed_grad):
    block_count = TOKENS // TOK_DEV

    def blocked(array):
        return array.astype(jnp.float32).reshape(block_count, TOK_DEV, HEADS, HD)
    query_blocks = blocked(query_rows)
    key_blocks = blocked(key_rows)
    value_blocks = blocked(value_rows)
    mask = causal_mask(TOK_DEV)

    def forward_step(state, inputs):
        query_block, key_block, value_block = inputs
        scores = jnp.einsum('thc,shc->hts', query_block, key_block, precision=highest) * mask
        attn_block = jnp.einsum('hts,shd->thd', scores, value_block, precision=highest)
        attn_block = attn_block + jnp.einsum('thc,hcd->thd', query_block, state, precision=highest)
        new_state = state + jnp.einsum('shc,shd->hcd', key_block, value_block, precision=highest)
        return (new_state, (attn_block, state))
    start_state = jnp.zeros((HEADS, HD, HD), jnp.float32)
    final_state, (attn_blocks, prev_states) = lax.scan(forward_step, start_state, (query_blocks, key_blocks, value_blocks))
    attn = attn_blocks.reshape(TOKENS, HEADS, HD)
    inv_rms = lax.rsqrt(lax.optimization_barrier(jnp.mean(attn * attn, axis=-1, keepdims=True)) + 1e-06)
    gain = norm_gain.astype(jnp.float32).reshape(HEADS, HD)
    normed = attn * inv_rms * gain
    sig = jax.nn.sigmoid(gate_input.astype(jnp.float32).reshape(TOKENS, HEADS, HD))
    out = (normed * sig).reshape(TOKENS, HEADS * HD).astype(jnp.bfloat16)
    mixed = jnp.dot(out, w_out, preferred_element_type=jnp.float32).astype(jnp.bfloat16)
    w_out_grad = jnp.dot(out.T, mixed_grad, preferred_element_type=jnp.float32)
    out_grad = jnp.dot(mixed_grad, w_out.T, preferred_element_type=jnp.float32).reshape(TOKENS, HEADS, HD)
    gate_grad = (out_grad * normed * sig * (1.0 - sig)).reshape(TOKENS, HEADS * HD).astype(jnp.bfloat16)
    scaled = out_grad * sig * gain
    attn_grad = inv_rms * scaled - inv_rms * inv_rms * inv_rms * attn * lax.optimization_barrier(jnp.mean(scaled * attn, axis=-1, keepdims=True))
    grad_blocks = attn_grad.reshape(block_count, TOK_DEV, HEADS, HD)

    def backward_step(later, inputs):
        query_block, key_block, value_block, prev_state, grad_block = inputs
        scores = jnp.einsum('thc,shc->hts', query_block, key_block, precision=highest) * mask
        prob_grad = jnp.einsum('thd,shd->hts', grad_block, value_block, precision=highest) * mask
        query_part = jnp.einsum('hts,shc->thc', prob_grad, key_block, precision=highest)
        query_part = query_part + jnp.einsum('thd,hcd->thc', grad_block, prev_state, precision=highest)
        key_part = jnp.einsum('hts,thc->shc', prob_grad, query_block, precision=highest)
        key_part = key_part + jnp.einsum('shd,hcd->shc', value_block, later, precision=highest)
        value_part = jnp.einsum('hts,thd->shd', scores, grad_block, precision=highest)
        value_part = value_part + jnp.einsum('shc,hcd->shd', key_block, later, precision=highest)
        new_later = later + jnp.einsum('thc,thd->hcd', query_block, grad_block, precision=highest)
        return (new_later, (query_part, key_part, value_part))
    first_later, (query_parts, key_parts, value_parts) = lax.scan(backward_step, start_state, (query_blocks, key_blocks, value_blocks, prev_states, grad_blocks), reverse=True)
    query_grad = query_parts.reshape(TOKENS, HEADS * HD).astype(jnp.bfloat16)
    key_grad = key_parts.reshape(TOKENS, HEADS * HD).astype(jnp.bfloat16)
    value_grad = value_parts.reshape(TOKENS, HEADS * HD).astype(jnp.bfloat16)
    return (mixed, w_out_grad, query_grad, key_grad, value_grad, gate_grad)
```

```python
import functools

import jax
import jax.numpy as jnp
from jax import lax
from jax.experimental import pallas as pl
from jax.experimental.pallas import tpu as pltpu
from jax.sharding import PartitionSpec as P

HD = 128
F32 = jnp.float32
BF16 = jnp.bfloat16
VMEM_LIMIT = 48 * 1024 * 1024

NT = (((1,), (1,)), ((), ()))
TN = (((0,), (0,)), ((), ()))
NN = (((1,), (0,)), ((), ()))


def dot(a, b, dims):
    return lax.dot_general(a, b, dims, preferred_element_type=F32)


def params():
    return pltpu.CompilerParams(vmem_limit_bytes=VMEM_LIMIT)


def cost(flops, nbytes):
    return pl.CostEstimate(flops=flops, bytes_accessed=nbytes, transcendentals=0)


def state_kernel(k_ref, v_ref, s_ref):
    s_ref[0] = dot(k_ref[...], v_ref[...], TN)


def block_states(keys, values):
    length, inner = keys.shape
    heads = inner // HD
    rows = pl.BlockSpec((length, HD), lambda i: (0, i))
    return pl.pallas_call(
        state_kernel,
        grid=(heads,),
        in_specs=[rows, rows],
        out_specs=pl.BlockSpec((1, HD, HD), lambda i: (i, 0, 0)),
        out_shape=jax.ShapeDtypeStruct((heads, HD, HD), F32),
        compiler_params=params(),
        cost_estimate=cost(2 * length * inner * HD, 4 * length * inner),
    )(keys, values)


def running_kernel(reverse, count, use_ref, p_ref, offset_ref, out_ref):
    total = offset_ref[...] * use_ref[0].astype(F32)
    for step in range(count):
        place = count - 1 - step if reverse else step
        out_ref[place] = total.astype(out_ref.dtype)
        if step < count - 1:
            total = total + p_ref[place]


def running_sum(pieces, offset, use, reverse):
    count, rows, lanes = pieces.shape
    return pl.pallas_call(
        functools.partial(running_kernel, reverse, count),
        in_specs=[
            pl.BlockSpec(memory_space=pltpu.SMEM),
            pl.BlockSpec(memory_space=pltpu.VMEM),
            pl.BlockSpec(memory_space=pltpu.VMEM),
        ],
        out_specs=pl.BlockSpec(memory_space=pltpu.VMEM),
        out_shape=jax.ShapeDtypeStruct((count, rows, lanes), BF16),
        compiler_params=params(),
        cost_estimate=cost(count * rows * lanes, 6 * count * rows * lanes),
    )(use, pieces, offset)


def head_grad_kernel(sel_ref, a_ref, b_ref, wa_ref, wb_ref, o_ref):
    total = dot(a_ref[...], wa_ref[...], NT) + dot(b_ref[...], wb_ref[...], NT)
    o_ref[...] = total.astype(o_ref.dtype)


def head_grad(sel, mine, other, w_mine, w_other, dtype):
    length, features = mine.shape
    tile = 512
    tiles = 1024 // tile
    whole = pl.BlockSpec((length, features), lambda j, s: (0, 0))
    return pl.pallas_call(
        head_grad_kernel,
        grid_spec=pltpu.PrefetchScalarGridSpec(
            num_scalar_prefetch=1,
            grid=(tiles,),
            in_specs=[
                whole,
                whole,
                pl.BlockSpec((tile, features), lambda j, s: ((s[0] * 2 + s[1]) * tiles + j, 0)),
                pl.BlockSpec((tile, features), lambda j, s: (s[0] * tiles + j, 0)),
            ],
            out_specs=pl.BlockSpec((length, tile), lambda j, s: (0, j)),
        ),
        out_shape=jax.ShapeDtypeStruct((length, 1024), dtype),
        compiler_params=params(),
        cost_estimate=cost(4 * length * features * 1024, 6 * 1024 * features),
    )(sel, mine, other, w_mine, w_other)


def score_rows(q_ref, k_ref, first, size):
    last = first + size
    scores = dot(q_ref[first:last], k_ref[:last], NT)
    return masked(scores, first)


def masked(scores, first):
    rows = lax.broadcasted_iota(jnp.int32, scores.shape, 0) + first
    cols = lax.broadcasted_iota(jnp.int32, scores.shape, 1)
    return jnp.where(cols <= rows, scores, 0.0).astype(BF16)


def head_kernel(
    part, q_ref, k_ref, v_ref, g_ref, gain_ref, s_ref, own_ref, far_ref,
    out_ref, gate_ref, hi_ref, lo_ref, state_ref,
):
    gain = gain_ref[...]
    length = q_ref.shape[0]
    for first in range(0, length, part):
        last = first + part
        scores = score_rows(q_ref, k_ref, first, part)
        attn = dot(scores, v_ref[:last], NN) + dot(q_ref[first:last], s_ref[0], NN)
        inv = lax.rsqrt(jnp.mean(attn * attn, axis=-1, keepdims=True) + 1e-06)
        normed = attn * inv * gain
        sig = 1.0 / (1.0 + jnp.exp(-g_ref[first:last].astype(F32)))
        out_ref[first:last] = (normed * sig).astype(BF16)
        grad = own_ref[first:last] + far_ref[first:last].astype(F32)
        gate_ref[first:last] = (grad * normed * sig * (1.0 - sig)).astype(BF16)
        scaled = grad * sig * gain
        mean = jnp.mean(scaled * attn, axis=-1, keepdims=True)
        full = inv * scaled - inv * inv * inv * attn * mean
        high = full.astype(BF16)
        hi_ref[first:last] = high
        lo_ref[first:last] = (full - high.astype(F32)).astype(BF16)
    state_ref[0] = dot(q_ref[...], hi_ref[...], TN)


def head_forward(queries, keys, values, gate, gain, state, own, far):
    length, inner = queries.shape
    heads = inner // HD
    rows = pl.BlockSpec((length, HD), lambda i: (0, i))
    square = pl.BlockSpec((1, HD, HD), lambda i: (i, 0, 0))
    wide = jax.ShapeDtypeStruct((length, inner), BF16)
    return pl.pallas_call(
        functools.partial(head_kernel, 256),
        grid=(heads,),
        in_specs=[
            rows, rows, rows, rows, pl.BlockSpec((1, HD), lambda i: (0, i)), square, rows, rows,
        ],
        out_specs=[rows, rows, rows, rows, square],
        out_shape=[wide, wide, wide, wide, jax.ShapeDtypeStruct((heads, HD, HD), F32)],
        compiler_params=params(),
        cost_estimate=cost(6 * length * length * inner, 20 * length * inner),
    )(queries, keys, values, gate, gain, state, own, far)


def grads_kernel(
    part, q_ref, k_ref, v_ref, hi_ref, lo_ref, s_ref, l_ref, dq_ref, dk_ref, dv_ref, dk_sum, dv_sum
):
    length = q_ref.shape[0]
    later = l_ref[0]
    dk_sum[...] = dot(v_ref[...], later, NT)
    dv_sum[...] = dot(k_ref[...], later, NN)
    for first in range(0, length, part):
        last = first + part
        high = hi_ref[first:last]
        scores = score_rows(q_ref, k_ref, first, part)
        prob = dot(high, v_ref[:last], NT) + dot(lo_ref[first:last], v_ref[:last], NT)
        prob = masked(prob, first)
        dq = dot(prob, k_ref[:last], NN) + dot(high, s_ref[0], NT)
        dq_ref[first:last] = dq.astype(BF16)
        dk_sum[:last] += dot(prob, q_ref[first:last], TN)
        dv_sum[:last] += dot(scores, high, TN)
    dk_ref[...] = dk_sum[...].astype(BF16)
    dv_ref[...] = dv_sum[...].astype(BF16)


def head_grads(queries, keys, values, high, low, state, later):
    length, inner = queries.shape
    heads = inner // HD
    rows = pl.BlockSpec((length, HD), lambda i: (0, i))
    square = pl.BlockSpec((1, HD, HD), lambda i: (i, 0, 0))
    wide = jax.ShapeDtypeStruct((length, inner), BF16)
    return pl.pallas_call(
        functools.partial(grads_kernel, 256),
        grid=(heads,),
        in_specs=[rows, rows, rows, rows, rows, square, square],
        out_specs=[rows, rows, rows],
        out_shape=[wide, wide, wide],
        scratch_shapes=[pltpu.VMEM((length, HD), F32), pltpu.VMEM((length, HD), F32)],
        compiler_params=params(),
        cost_estimate=cost(12 * length * length * inner, 16 * length * inner),
    )(queries, keys, values, high, low, state, later)


def mixed_kernel(sel_ref, a_ref, b_ref, c_ref, d_ref, w_ref, o_ref):
    total = None
    for place, block in enumerate((a_ref, b_ref, c_ref, d_ref)):
        first = pl.multiple_of(sel_ref[place] * 1024, 1024)
        term = dot(block[...], w_ref[pl.ds(first, 1024), :], NN)
        total = term if total is None else total + term
    o_ref[...] = total.astype(BF16)


def mix(sel, blocks, w_out):
    length, width = blocks[0].shape
    inner, features = w_out.shape
    tile = 256
    whole = pl.BlockSpec((length, width), lambda j, s: (0, 0))
    return pl.pallas_call(
        mixed_kernel,
        grid_spec=pltpu.PrefetchScalarGridSpec(
            num_scalar_prefetch=1,
            grid=(features // tile,),
            in_specs=[whole] * 4 + [pl.BlockSpec((inner, tile), lambda j, s: (0, j))],
            out_specs=pl.BlockSpec((length, tile), lambda j, s: (0, j)),
        ),
        out_shape=jax.ShapeDtypeStruct((length, features), BF16),
        compiler_params=params(),
        cost_estimate=cost(2 * length * inner * features, 2 * inner * features),
    )(sel, *blocks, w_out)


def weight_kernel(sel_ref, a0_ref, a1_ref, b0_ref, b1_ref, m0_ref, m1_ref, o_ref):
    source = pl.program_id(0)

    @pl.when(source == 0)
    def _():
        total = dot(a0_ref[...], m0_ref[...], TN) + dot(a1_ref[...], m1_ref[...], TN)
        o_ref[...] = total.astype(BF16)

    @pl.when(source == 1)
    def _():
        total = dot(b0_ref[...], m0_ref[...], TN) + dot(b1_ref[...], m1_ref[...], TN)
        o_ref[...] = total.astype(BF16)


def weight_grad(sel, mine, other, grads):
    length, width = mine[0].shape
    features = grads[0].shape[1]
    tile = 256
    tiles = width // tile
    last = tiles - 1
    first_rows = pl.BlockSpec((length, tile), lambda i, j, s: (0, jnp.where(i == 0, j, last)))
    second_rows = pl.BlockSpec((length, tile), lambda i, j, s: (0, jnp.where(i == 0, 0, j)))
    whole = pl.BlockSpec((length, features), lambda i, j, s: (0, 0))
    return pl.pallas_call(
        weight_kernel,
        grid_spec=pltpu.PrefetchScalarGridSpec(
            num_scalar_prefetch=1,
            grid=(2, tiles),
            in_specs=[first_rows, first_rows, second_rows, second_rows, whole, whole],
            out_specs=pl.BlockSpec(
                (tile, features), lambda i, j, s: ((s[0] + i - 2 * s[0] * i) * tiles + j, 0)
            ),
        ),
        out_shape=jax.ShapeDtypeStruct((2 * width, features), BF16),
        compiler_params=params(),
        cost_estimate=cost(8 * length * width * features, 4 * width * features),
    )(sel, mine[0], mine[1], other[0], other[1], *grads)


def per_device(query_rows, key_rows, value_rows, gate_input, norm_gain, w_out, mixed_grad):
    length, inner_dev = query_rows.shape
    heads_dev = inner_dev // HD
    features = w_out.shape[1]
    planes, across = 2, 16
    ctx, fsdp = lax.axis_index("ctx"), lax.axis_index("fsdp")
    y_lo = ctx // across
    y_hi, core = fsdp // 2, fsdp % 2
    groups = [[y * across + i for i in range(across)] for y in range(planes)]
    core_swap = [(0, 1), (1, 0), (2, 3), (3, 2)]
    hi_swap = [(0, 2), (1, 3), (2, 0), (3, 1)]
    lo_swap = [(i, (i + across) % (2 * across)) for i in range(2 * across)]

    def swap_core(array):
        return lax.ppermute(array, "fsdp", core_swap)

    def swap_hi(array):
        return lax.ppermute(array, "fsdp", hi_swap)

    def swap_lo(array):
        return lax.ppermute(array, "ctx", lo_swap)

    def exchange(array):
        return lax.all_to_all(array, "ctx", 0, 0, axis_index_groups=groups)

    def states_before(local, reverse):
        rows = heads_dev * HD // across
        pieces = exchange(local.reshape(across, rows, HD))
        offset = swap_lo(jnp.sum(pieces, axis=0))
        use = (y_lo == (0 if reverse else 1)).astype(jnp.int32).reshape(1)
        sums = running_sum(pieces, offset, use, reverse)
        return exchange(sums).reshape(heads_dev, HD, HD)

    grad_pair = swap_lo(mixed_grad)
    grad_core = swap_core(mixed_grad)
    w_rows = w_out.reshape(2, 2, inner_dev, features)
    w_sent = lax.dynamic_index_in_dim(w_rows, 1 - core, 1, False).reshape(2 * inner_dev, features)
    w_core = swap_core(w_sent)
    select_far = jnp.stack([1 - y_hi, core]).astype(jnp.int32)
    select_own = jnp.stack([y_hi, core]).astype(jnp.int32)
    far_part = head_grad(select_far, mixed_grad, grad_core, w_out, w_core, BF16)
    grad_own = head_grad(select_own, mixed_grad, grad_core, w_out, w_core, F32)

    local_state = block_states(key_rows, value_rows)
    prev_state = states_before(local_state, False)
    grad_far = swap_hi(far_part)

    out, gate_grad, high, low, grad_state = head_forward(
        query_rows, key_rows, value_rows, gate_input, norm_gain.reshape(1, inner_dev),
        prev_state, grad_own, grad_far,
    )

    moves = []
    for turn in range(2):
        pairs = []
        for place in range(2 * across):
            lo, rest = place // across, place % across
            for part in range(4):
                hi, side = part // 2, part % 2
                target = (hi * across + rest) * 4 + (lo ^ turn) * 2 + side
                pairs.append((place * 4 + part, target))
        moves.append(lax.ppermute(out, ("ctx", "fsdp"), pairs))
    moved_core = [swap_core(block) for block in moves]
    near = y_hi == y_lo
    grads = [jnp.where(near, mixed_grad, grad_pair), jnp.where(near, grad_pair, mixed_grad)]
    weight = weight_grad(core.astype(jnp.int32).reshape(1), moves, moved_core, grads)
    parts = exchange(weight.reshape(across, 2 * inner_dev // across, features))
    w_out_grad = jnp.sum(parts.astype(F32), axis=0)

    out_far = swap_hi(out)
    blocks = [out, swap_core(out), out_far, swap_core(out_far)]
    order = jnp.stack(
        [fsdp, fsdp + 1 - 2 * core, (fsdp + 2) % 4, (fsdp + 2) % 4 + 1 - 2 * core]
    ).astype(jnp.int32)
    mixed = mix(order, blocks, w_out)

    later_state = states_before(grad_state, True)
    query_grad, key_grad, value_grad = head_grads(
        query_rows, key_rows, value_rows, high, low, prev_state, later_state
    )
    return (mixed, w_out_grad, query_grad, key_grad, value_grad, gate_grad)


def solution(mesh):
    return jax.shard_map(
        per_device,
        mesh=mesh,
        in_specs=(
            P("ctx", "fsdp"),
            P("ctx", "fsdp"),
            P("ctx", "fsdp"),
            P("ctx", "fsdp"),
            P("fsdp"),
            P(None, "fsdp"),
            P("ctx", "fsdp"),
        ),
        out_specs=(
            P("ctx", "fsdp"),
            P("ctx", "fsdp"),
            P("ctx", "fsdp"),
            P("ctx", "fsdp"),
            P("ctx", "fsdp"),
            P("ctx", "fsdp"),
        ),
        check_vma=False,
    )
```

```python
import functools

import jax
import jax.numpy as jnp
from jax import lax
from jax.experimental import pallas as pl
from jax.experimental.pallas import tpu as pltpu
from jax.sharding import PartitionSpec as P

HD = 128
F32 = jnp.float32
BF16 = jnp.bfloat16
VMEM_LIMIT = 62 * 1024 * 1024

NT = (((1,), (1,)), ((), ()))
TN = (((0,), (0,)), ((), ()))
NN = (((1,), (0,)), ((), ()))


def dot(a, b, dims):
    return lax.dot_general(a, b, dims, preferred_element_type=F32)


def after(array, other):
    return lax.optimization_barrier((array, other))[0]


def params():
    return pltpu.CompilerParams(vmem_limit_bytes=VMEM_LIMIT)


def cost(flops, nbytes):
    return pl.CostEstimate(flops=flops, bytes_accessed=nbytes, transcendentals=0)


def state_kernel(k_ref, v_ref, s_ref):
    for head in range(2):
        cols = slice(head * HD, (head + 1) * HD)
        s_ref[head] = dot(k_ref[:, cols], v_ref[:, cols], TN)


def block_states(keys, values):
    length, inner = keys.shape
    heads = inner // HD
    rows = pl.BlockSpec((length, 2 * HD), lambda i: (0, i))
    return pl.pallas_call(
        state_kernel,
        grid=(heads // 2,),
        in_specs=[rows, rows],
        out_specs=pl.BlockSpec((2, HD, HD), lambda i: (i, 0, 0)),
        out_shape=jax.ShapeDtypeStruct((heads, HD, HD), F32),
        compiler_params=params(),
        cost_estimate=cost(2 * length * inner * HD, 4 * length * inner),
    )(keys, values)


def running_kernel(reverse, count, use_ref, p_ref, offset_ref, *rest):
    out_ref = rest[-1]
    rows, lanes = out_ref.shape[1], p_ref.shape[2]
    groups = p_ref.shape[1] // rows
    if out_ref.shape[2] > groups * lanes:
        out_ref[...] = jnp.zeros(out_ref.shape, out_ref.dtype)
    total = offset_ref[...] * use_ref[0].astype(F32)
    for step in range(count):
        place = count - 1 - step if reverse else step
        piece = total.astype(out_ref.dtype)
        for group in range(groups):
            cols = slice(group * lanes, (group + 1) * lanes)
            out_ref[place, :, cols] = piece[group * rows : (group + 1) * rows]
        if step < count - 1:
            total = total + p_ref[place]


def running_sum(pieces, offset, use, reverse, target=None):
    count, rows, lanes = pieces.shape
    in_specs = [
        pl.BlockSpec(memory_space=pltpu.SMEM),
        pl.BlockSpec(pieces.shape, lambda i: (0, 0, 0)),
        pl.BlockSpec(offset.shape, lambda i: (0, 0)),
    ]
    operands = [use, pieces, offset]
    if target is None:
        aliases = {}
        out_spec = pl.BlockSpec(pieces.shape, lambda i: (0, 0, 0))
        out_shape = jax.ShapeDtypeStruct(pieces.shape, BF16)
    else:
        aliases = {3: 0}
        in_specs.append(pl.BlockSpec(memory_space=pl.ANY))
        operands.append(target)
        last = target.shape[1] // 16 - 1
        out_spec = pl.BlockSpec((count, 16, target.shape[2]), lambda i: (0, last, 0))
        out_shape = jax.ShapeDtypeStruct(target.shape, BF16)
    return pl.pallas_call(
        functools.partial(running_kernel, reverse, count),
        grid=(1,),
        in_specs=in_specs,
        out_specs=out_spec,
        out_shape=out_shape,
        input_output_aliases=aliases,
        compiler_params=params(),
        cost_estimate=cost(count * rows * lanes, 6 * count * rows * lanes),
    )(*operands)


def head_term_kernel(sel_ref, a_ref, w_ref, o_ref):
    o_ref[...] = dot(a_ref[...], w_ref[...], NT).astype(o_ref.dtype)


def head_sum_kernel(sel_ref, a_ref, w_ref, r_ref, o_ref):
    total = dot(a_ref[...], w_ref[...], NT) + r_ref[...].astype(F32)
    o_ref[...] = total.astype(o_ref.dtype)


def head_term(place, grad, w_out, width, dtype, received=None):
    length, features = grad.shape
    tile = 512
    tiles = width // tile
    rows = pl.BlockSpec((length, tile), lambda j, s: (0, j))
    in_specs = [
        pl.BlockSpec((length, features), lambda j, s: (0, 0)),
        pl.BlockSpec((tile, features), lambda j, s: (s[0] * tiles + j, 0)),
    ]
    operands = [place.astype(jnp.int32).reshape(1), grad, w_out]
    if received is not None:
        in_specs.append(rows)
        operands.append(received)
    return pl.pallas_call(
        head_term_kernel if received is None else head_sum_kernel,
        grid_spec=pltpu.PrefetchScalarGridSpec(
            num_scalar_prefetch=1, grid=(tiles,), in_specs=in_specs, out_specs=rows
        ),
        out_shape=jax.ShapeDtypeStruct((length, width), dtype),
        compiler_params=params(),
        cost_estimate=cost(2 * length * features * width, 4 * width * features),
    )(*operands)


def score_rows(q_ref, k_ref, first, size):
    last = first + size
    scores = dot(q_ref[first:last], k_ref[:last], NT)
    return masked(scores, first)


def masked(scores, first):
    rows = lax.broadcasted_iota(jnp.int32, scores.shape, 0) + first
    cols = lax.broadcasted_iota(jnp.int32, scores.shape, 1)
    return jnp.where(cols <= rows, scores, 0.0).astype(BF16)


def sigmoid(gate):
    return 0.5 * jnp.tanh(0.5 * gate.astype(F32)) + 0.5


def head_out_kernel(
    part, half_ref, q_ref, k_ref, v_ref, g_ref, gain_ref, s_ref, mine_ref, other_ref, attn_ref
):
    length = q_ref.shape[0]
    half = HD // 2
    lane = lax.broadcasted_iota(jnp.int32, (part, HD), 1)
    upper = half_ref[0] == 1
    for first in range(0, length, part):
        last = first + part
        outs = []
        for head in range(2):
            cols = slice(head * HD, (head + 1) * HD)
            queries = q_ref[first:last, cols]
            scores = masked(dot(queries, k_ref[:last, cols], NT), first)
            attn = dot(scores, v_ref[:last, cols], NN) + dot(queries, s_ref[head], NN)
            inv = lax.rsqrt(jnp.mean(attn * attn, axis=-1, keepdims=True) + 1e-06)
            outs.append(attn * inv * gain_ref[:, cols] * sigmoid(g_ref[first:last, cols]))
            attn_ref[first:last, cols] = attn
        low = jnp.where(lane < half, outs[0], pltpu.roll(outs[1], half, 1))
        high = jnp.where(lane < half, pltpu.roll(outs[0], half, 1), outs[1])
        mine_ref[first:last] = jnp.where(upper, high, low).astype(BF16)
        other_ref[first:last] = jnp.where(upper, low, high).astype(BF16)


def head_outputs(half, queries, keys, values, gate, gain, state):
    length, inner = queries.shape
    heads = inner // HD
    rows = pl.BlockSpec((length, 2 * HD), lambda i: (0, i))
    packed_rows = pl.BlockSpec((length, HD), lambda i: (0, i))
    square = pl.BlockSpec((2, HD, HD), lambda i: (i, 0, 0))
    packed = jax.ShapeDtypeStruct((length, inner // 2), BF16)
    return pl.pallas_call(
        functools.partial(head_out_kernel, 256),
        grid=(heads // 2,),
        in_specs=[
            pl.BlockSpec(memory_space=pltpu.SMEM),
            rows,
            rows,
            rows,
            rows,
            pl.BlockSpec((1, 2 * HD), lambda i: (0, i)),
            square,
        ],
        out_specs=[packed_rows, packed_rows, rows],
        out_shape=[packed, packed, jax.ShapeDtypeStruct((length, inner), F32)],
        compiler_params=params(),
        cost_estimate=cost(4 * length * length * inner, 14 * length * inner),
    )(half, queries, keys, values, gate, gain, state)


def head_back_kernel(
    q_ref, g_ref, gain_ref, attn_ref, own_ref, far_ref, gate_ref, hi_ref, lo_ref, state_ref
):
    gain = gain_ref[...]
    attn = attn_ref[...]
    inv = lax.rsqrt(jnp.mean(attn * attn, axis=-1, keepdims=True) + 1e-06)
    sig = sigmoid(g_ref[...])
    grad = own_ref[...] + far_ref[...].astype(F32)
    unit = attn * inv
    scaled = grad * sig * gain
    product = scaled * unit
    gate_ref[...] = (product * (1.0 - sig)).astype(BF16)
    full = inv * (scaled - unit * jnp.mean(product, axis=-1, keepdims=True))
    high = full.astype(BF16)
    hi_ref[...] = high
    lo_ref[...] = (full - high.astype(F32)).astype(BF16)
    state_ref[0] = dot(q_ref[...], high, TN)


def head_back(queries, gate, gain, attn, own, far):
    length, inner = queries.shape
    heads = inner // HD
    rows = pl.BlockSpec((length, HD), lambda i: (0, i))
    square = pl.BlockSpec((1, HD, HD), lambda i: (i, 0, 0))
    wide = jax.ShapeDtypeStruct((length, inner), BF16)
    return pl.pallas_call(
        head_back_kernel,
        grid=(heads,),
        in_specs=[rows, rows, pl.BlockSpec((1, HD), lambda i: (0, i)), rows, rows, rows],
        out_specs=[rows, rows, rows, square],
        out_shape=[wide, wide, wide, jax.ShapeDtypeStruct((heads, HD, HD), F32)],
        compiler_params=params(),
        cost_estimate=cost(2 * length * HD * inner, 20 * length * inner),
    )(queries, gate, gain, attn, own, far)


def grads_kernel(
    part, q_ref, k_ref, v_ref, hi_ref, lo_ref, s_ref, dq_ref, dk_ref, dv_ref
):
    length = q_ref.shape[0]
    for first in range(0, length, part):
        last = first + part
        high = hi_ref[first:last]
        scores = score_rows(q_ref, k_ref, first, part)
        prob = dot(high, v_ref[:last], NT) + dot(lo_ref[first:last], v_ref[:last], NT)
        prob = masked(prob, first)
        dq = dot(prob, k_ref[:last], NN) + dot(high, s_ref[0], NT)
        dq_ref[first:last] = dq.astype(BF16)
        dk = dot(prob, q_ref[first:last], TN)
        dv = dot(scores, high, TN)
        if first:
            dk_ref[:first] += dk[:first]
            dv_ref[:first] += dv[:first]
        dk_ref[first:last] = dk[first:]
        dv_ref[first:last] = dv[first:]


def head_grads(queries, keys, values, high, low, state):
    length, inner = queries.shape
    heads = inner // HD
    rows = pl.BlockSpec((length, HD), lambda i: (0, i))
    square = pl.BlockSpec((1, HD, HD), lambda i: (i, 0, 0))
    wide = jax.ShapeDtypeStruct((length, inner), BF16)
    full = jax.ShapeDtypeStruct((length, inner), F32)
    return pl.pallas_call(
        functools.partial(grads_kernel, 256),
        grid=(heads,),
        in_specs=[rows, rows, rows, rows, rows, square],
        out_specs=[rows, rows, rows],
        out_shape=[wide, full, full],
        compiler_params=params(),
        cost_estimate=cost(10 * length * length * inner, 20 * length * inner),
    )(queries, keys, values, high, low, state)


def later_kernel(k_ref, v_ref, dk_ref, dv_ref, l_ref, dk_out, dv_out):
    groups = HD // (2 * l_ref.shape[1])
    for head in range(2):
        cols = slice(head * HD, (head + 1) * HD)
        later = jnp.concatenate(
            [
                l_ref[2 * head + piece, :, group * HD : (group + 1) * HD]
                for piece in range(2)
                for group in range(groups)
            ],
            axis=0,
        )
        dk_out[:, cols] = (dk_ref[:, cols] + dot(v_ref[:, cols], later, NT)).astype(BF16)
        dv_out[:, cols] = (dv_ref[:, cols] + dot(k_ref[:, cols], later, NN)).astype(BF16)


def later_grads(keys, values, key_part, value_part, parts):
    length, inner = keys.shape
    heads = inner // HD
    rows = pl.BlockSpec((length, 2 * HD), lambda i: (0, i))
    wide = jax.ShapeDtypeStruct((length, inner), BF16)
    last = parts.shape[1] // 16 - 1
    return pl.pallas_call(
        later_kernel,
        grid=(heads // 2,),
        in_specs=[
            rows,
            rows,
            rows,
            rows,
            pl.BlockSpec((4, 16, parts.shape[2]), lambda i: (i, last, 0)),
        ],
        out_specs=[rows, rows],
        out_shape=[wide, wide],
        compiler_params=params(),
        cost_estimate=cost(4 * length * HD * inner, 16 * length * inner),
    )(keys, values, key_part, value_part, parts)


def mixed_kernel(sel_ref, *refs):
    blocks, w_ref, o_ref = refs[:-2], refs[-2], refs[-1]
    half = HD // 2
    total = None
    for place, block in enumerate(blocks):
        rows = []
        for head in range(block.shape[1] // half):
            first = sel_ref[2 * place] * 1024 + sel_ref[2 * place + 1] * half + head * HD
            rows.append(w_ref[pl.ds(pl.multiple_of(first, half), half), :])
        term = dot(block[...], jnp.concatenate(rows, axis=0), NN)
        total = term if total is None else total + term
    o_ref[...] = total.astype(BF16)


def mix(sel, blocks, w_out):
    length, width = blocks[0].shape
    inner, features = w_out.shape
    tile = 256
    whole = pl.BlockSpec((length, width), lambda j, s: (0, 0))
    return pl.pallas_call(
        mixed_kernel,
        grid_spec=pltpu.PrefetchScalarGridSpec(
            num_scalar_prefetch=1,
            grid=(features // tile,),
            in_specs=[whole] * len(blocks) + [pl.BlockSpec((inner, tile), lambda j, s: (0, j))],
            out_specs=pl.BlockSpec((length, tile), lambda j, s: (0, j)),
        ),
        out_shape=jax.ShapeDtypeStruct((length, features), BF16),
        compiler_params=params(),
        cost_estimate=cost(2 * length * inner * features, 2 * inner * features),
    )(sel, *blocks, w_out)


def weight_kernel(sel_ref, a0_ref, a1_ref, b0_ref, b1_ref, m0_ref, m1_ref, *rest):
    o_ref = rest[-1]
    count, size = o_ref.shape[:2]
    for source, (first, second) in enumerate(((a0_ref, a1_ref), (b0_ref, b1_ref))):

        @pl.when(pl.program_id(0) == source)
        def _(first=first, second=second):
            total = dot(first[...], m0_ref[...], TN) + dot(second[...], m1_ref[...], TN)
            for piece in range(count):
                o_ref[piece] = total[piece * size : (piece + 1) * size].astype(BF16)


def weight_grad(sel, mine, other, grads, across, index, target=None):
    length, width = mine[0].shape
    features = grads[0].shape[1]
    size = 2 * width // across
    tile = 256
    tiles, count = width // tile, tile // size
    last = tiles - 1

    def place(i, j, s):
        return ((s[0] + i - 2 * s[0] * i) * tiles + j, index, 0)

    first_rows = pl.BlockSpec((length, tile), lambda i, j, s: (0, jnp.where(i == 0, j, last)))
    second_rows = pl.BlockSpec((length, tile), lambda i, j, s: (0, jnp.where(i == 0, 0, j)))
    whole = pl.BlockSpec((length, features), lambda i, j, s: (0, 0))
    in_specs = [first_rows, first_rows, second_rows, second_rows, whole, whole]
    operands = [sel, mine[0], mine[1], other[0], other[1], *grads]
    aliases = {}
    if target is not None:
        in_specs.append(pl.BlockSpec(memory_space=pl.ANY))
        operands.append(target)
        aliases = {len(operands) - 1: 0}
    return pl.pallas_call(
        weight_kernel,
        grid_spec=pltpu.PrefetchScalarGridSpec(
            num_scalar_prefetch=1,
            grid=(2, tiles),
            in_specs=in_specs,
            out_specs=pl.BlockSpec((count, size, features), place),
        ),
        out_shape=jax.ShapeDtypeStruct((across, 2 * size + 16, features), BF16),
        input_output_aliases=aliases,
        compiler_params=params(),
        cost_estimate=cost(8 * length * width * features, 4 * width * features),
    )(*operands)


def per_device(query_rows, key_rows, value_rows, gate_input, norm_gain, w_out, mixed_grad):
    length, inner_dev = query_rows.shape
    heads_dev = inner_dev // HD
    features = w_out.shape[1]
    planes, across = 2, 16
    ctx, fsdp = lax.axis_index("ctx"), lax.axis_index("fsdp")
    y_lo = ctx // across
    y_hi, core = fsdp // 2, fsdp % 2
    groups = [[y * across + i for i in range(across)] for y in range(planes)]
    core_swap = [(0, 1), (1, 0), (2, 3), (3, 2)]
    hi_swap = [(0, 2), (1, 3), (2, 0), (3, 1)]
    lo_swap = [(i, (i + across) % (2 * across)) for i in range(2 * across)]

    def swap_core(array):
        return lax.ppermute(array, "fsdp", core_swap)

    def swap_hi(array):
        return lax.ppermute(array, "fsdp", hi_swap)

    def swap_lo(array):
        return lax.ppermute(array, "ctx", lo_swap)

    def exchange(array):
        return lax.all_to_all(array, "ctx", 0, 0, axis_index_groups=groups)

    def sums_before(pieces, offset, reverse, target=None):
        use = (y_lo == (0 if reverse else 1)).astype(jnp.int32).reshape(1)
        return running_sum(pieces, offset, use, reverse, target)

    def split_states(local):
        return exchange(local.reshape(across, heads_dev * HD // across, HD))

    gain = norm_gain.reshape(1, inner_dev)
    peer, far = fsdp + 1 - 2 * core, (fsdp + 2) % 4
    far_peer = (peer + 2) % 4

    grad_pair = swap_lo(mixed_grad)
    local_state = block_states(key_rows, value_rows)
    pieces = split_states(local_state)
    far_sent = head_term(after(far_peer, local_state), mixed_grad, w_out, inner_dev, BF16)
    far_got = swap_core(far_sent)
    far_part = head_term(far, mixed_grad, w_out, inner_dev, BF16, far_got)
    own_sent = head_term(after(peer, far_got), mixed_grad, w_out, inner_dev, BF16)
    own_got = swap_core(own_sent)
    total = jnp.sum(after(after(pieces, far_part), own_sent), axis=0)
    offset = swap_lo(total)
    grad_far = swap_hi(after(after(far_part, offset), grad_pair))
    sums = sums_before(pieces, offset, False)
    grad_own = head_term(after(fsdp, sums), mixed_grad, w_out, inner_dev, F32, own_got)
    prev_state = exchange(sums).reshape(heads_dev, HD, HD)

    half = y_lo.astype(jnp.int32).reshape(1)
    out, out_other, attn = head_outputs(
        half, after(query_rows, grad_own), key_rows, value_rows, gate_input, gain, prev_state
    )
    gate_grad, high, low, grad_state = head_back(
        query_rows, gate_input, gain, attn, grad_own, grad_far
    )
    later_pieces = split_states(grad_state)
    later_total = jnp.sum(later_pieces, axis=0)

    across_y = []
    for place in range(2 * across):
        for part in range(4):
            target = ((place + across) % (2 * across)) * 4 + (part + 2) % 4
            across_y.append((place * 4 + part, target))
    out_pair = swap_lo(out_other)
    out_far = swap_hi(out)
    out_far_pair = lax.ppermute(out_other, ("ctx", "fsdp"), across_y)
    out_core, out_pair_core = swap_core(out), swap_core(after(out_pair, grad_state))
    select = core.astype(jnp.int32).reshape(1)
    grads = [mixed_grad, grad_pair]
    out_far_core, out_far_pair_core = swap_core(out_far), swap_core(out_far_pair)
    weight = weight_grad(
        after(select, later_total), [out, out_pair], [out_core, out_pair_core], grads, across, 0
    )
    weight = weight_grad(
        select, [out_far, out_far_pair], [out_far_core, out_far_pair_core], grads, across, 1,
        weight,
    )
    later_offset = swap_lo(later_total)
    weight = sums_before(later_pieces, later_offset, True, weight)
    parts = exchange(weight)
    far_other = swap_hi(after(out_other, later_offset))
    query_grad, key_part, value_part = head_grads(
        after(query_rows, weight), key_rows, value_rows, high, low, prev_state
    )

    blocks = [out, out_other, out_core, swap_core(after(out_other, later_offset))]
    blocks += [out_far, far_other, out_far_core, swap_core(far_other)]
    order = []
    for heads in (fsdp, peer, far, far_peer):
        order += [heads, y_lo, heads, 1 - y_lo]
    order = jnp.stack(order).astype(jnp.int32)
    mixed = mix(after(order, query_grad), blocks, w_out)

    parts = after(parts, mixed)
    key_grad, value_grad = later_grads(key_rows, value_rows, key_part, value_part, parts)
    size = 2 * inner_dev // (2 * across)
    near_sum = jnp.sum(parts[:, :size].astype(F32), axis=0)
    far_sum = jnp.sum(parts[:, size : 2 * size].astype(F32), axis=0)
    keeps = y_hi == y_lo
    kept = jnp.where(keeps, near_sum, far_sum)
    received = swap_lo(jnp.where(keeps, far_sum, near_sum))
    w_out_grad = jnp.where(
        y_lo == 0,
        jnp.concatenate([kept, received], axis=0),
        jnp.concatenate([received, kept], axis=0),
    )
    return (mixed, w_out_grad, query_grad, key_grad, value_grad, gate_grad)


def solution(mesh):
    return jax.shard_map(
        per_device,
        mesh=mesh,
        in_specs=(
            P("ctx", "fsdp"),
            P("ctx", "fsdp"),
            P("ctx", "fsdp"),
            P("ctx", "fsdp"),
            P("fsdp"),
            P(None, "fsdp"),
            P("ctx", "fsdp"),
        ),
        out_specs=(
            P("ctx", "fsdp"),
            P("ctx", "fsdp"),
            P("ctx", "fsdp"),
            P("ctx", "fsdp"),
            P("ctx", "fsdp"),
            P("ctx", "fsdp"),
        ),
        check_vma=False,
    )
```

```python
import functools

import jax
import jax.numpy as jnp
from jax import lax
from jax.experimental import pallas as pl
from jax.experimental.pallas import tpu as pltpu
from jax.sharding import PartitionSpec as P

HD = 128
F32 = jnp.float32
BF16 = jnp.bfloat16
VMEM_LIMIT = 62 * 1024 * 1024

NT = (((1,), (1,)), ((), ()))
TN = (((0,), (0,)), ((), ()))
NN = (((1,), (0,)), ((), ()))


def dot(a, b, dims):
    return lax.dot_general(a, b, dims, preferred_element_type=F32)


def after(array, *others):
    return lax.optimization_barrier((array,) + others)[0]


def tied(kernel, operands, in_specs, deps):
    count = len(operands)

    def run(*refs):
        kernel(*refs[:count], *refs[count + len(deps) :])

    specs = [pl.BlockSpec(memory_space=pl.ANY)] * len(deps)
    return run, list(operands) + list(deps), list(in_specs) + specs


def params():
    return pltpu.CompilerParams(vmem_limit_bytes=VMEM_LIMIT)


def cost(flops, nbytes):
    return pl.CostEstimate(flops=flops, bytes_accessed=nbytes, transcendentals=0)


def state_kernel(k_ref, v_ref, s_ref):
    for head in range(s_ref.shape[0]):
        cols = slice(head * HD, (head + 1) * HD)
        s_ref[head] = dot(k_ref[:, cols], v_ref[:, cols], TN)


def block_states(keys, values):
    length, inner = keys.shape
    heads = inner // HD
    step = 4
    rows = pl.BlockSpec((length, step * HD), lambda i: (0, i))
    return pl.pallas_call(
        state_kernel,
        grid=(heads // step,),
        in_specs=[rows, rows],
        out_specs=pl.BlockSpec((step, HD, HD), lambda i: (i, 0, 0)),
        out_shape=jax.ShapeDtypeStruct((heads, HD, HD), F32),
        compiler_params=params(),
        cost_estimate=cost(2 * length * inner * HD, 4 * length * inner),
    )(keys, values)


def running_kernel(reverse, count, use_ref, p_ref, offset_ref, *rest):
    out_ref = rest[-1]
    rows, lanes = out_ref.shape[1], p_ref.shape[2]
    groups = p_ref.shape[1] // rows
    if out_ref.shape[2] > groups * lanes:
        out_ref[...] = jnp.zeros(out_ref.shape, out_ref.dtype)
    total = offset_ref[...] * use_ref[0].astype(F32)
    for step in range(count):
        place = count - 1 - step if reverse else step
        piece = total.astype(out_ref.dtype)
        for group in range(groups):
            cols = slice(group * lanes, (group + 1) * lanes)
            out_ref[place, :, cols] = piece[group * rows : (group + 1) * rows]
        if step < count - 1:
            total = total + p_ref[place]


def running_sum(pieces, offset, use, reverse, target=None, deps=()):
    count, rows, lanes = pieces.shape
    in_specs = [
        pl.BlockSpec(memory_space=pltpu.SMEM),
        pl.BlockSpec(pieces.shape, lambda i: (0, 0, 0)),
        pl.BlockSpec(offset.shape, lambda i: (0, 0)),
    ]
    operands = [use, pieces, offset]
    if target is None:
        aliases = {}
        out_spec = pl.BlockSpec(pieces.shape, lambda i: (0, 0, 0))
        out_shape = jax.ShapeDtypeStruct(pieces.shape, BF16)
    else:
        aliases = {3: 0}
        in_specs.append(pl.BlockSpec(memory_space=pl.ANY))
        operands.append(target)
        last = target.shape[1] // 16 - 1
        out_spec = pl.BlockSpec((count, 16, target.shape[2]), lambda i: (0, last, 0))
        out_shape = jax.ShapeDtypeStruct(target.shape, BF16)
    kernel = functools.partial(running_kernel, reverse, count)
    kernel, operands, in_specs = tied(kernel, operands, in_specs, deps)
    return pl.pallas_call(
        kernel,
        grid=(1,),
        in_specs=in_specs,
        out_specs=out_spec,
        out_shape=out_shape,
        input_output_aliases=aliases,
        compiler_params=params(),
        cost_estimate=cost(count * rows * lanes, 6 * count * rows * lanes),
    )(*operands)


def head_term_kernel(sel_ref, a_ref, w_ref, o_ref):
    o_ref[0] = dot(a_ref[...], w_ref[...], NT).astype(o_ref.dtype)


def head_sum_kernel(sel_ref, a_ref, w_ref, r_ref, o_ref):
    total = dot(a_ref[...], w_ref[...], NT) + r_ref[0].astype(F32)
    o_ref[0] = total.astype(o_ref.dtype)


def head_term(places, grad, w_out, width, dtype, received=None, part=0):
    length, features = grad.shape
    count = len(places)
    tile = 512 if count == 1 else width
    tiles = width // tile
    in_specs = [
        pl.BlockSpec((length, features), lambda i, j, s: (0, 0)),
        pl.BlockSpec((tile, features), lambda i, j, s: (s[i] * tiles + j, 0)),
    ]
    operands = [jnp.stack(places).astype(jnp.int32), grad, w_out]
    if received is not None:
        in_specs.append(pl.BlockSpec((1, length, tile), lambda i, j, s: (part, 0, j)))
        operands.append(received)
    return pl.pallas_call(
        head_term_kernel if received is None else head_sum_kernel,
        grid_spec=pltpu.PrefetchScalarGridSpec(
            num_scalar_prefetch=1,
            grid=(count, tiles),
            in_specs=in_specs,
            out_specs=pl.BlockSpec((1, length, tile), lambda i, j, s: (i, 0, j)),
        ),
        out_shape=jax.ShapeDtypeStruct((count, length, width), dtype),
        compiler_params=params(),
        cost_estimate=cost(2 * length * features * width, 4 * width * features),
    )(*operands)


def score_rows(q_ref, k_ref, first, size):
    last = first + size
    scores = dot(q_ref[first:last], k_ref[:last], NT)
    return masked(scores, first)


def masked(scores, first):
    rows = lax.broadcasted_iota(jnp.int32, scores.shape, 0) + first
    cols = lax.broadcasted_iota(jnp.int32, scores.shape, 1)
    return jnp.where(cols <= rows, scores, 0.0).astype(BF16)


def sigmoid(gate):
    return 0.5 * jnp.tanh(0.5 * gate.astype(F32)) + 0.5


def head_out_kernel(
    part, half_ref, q_ref, k_ref, v_ref, g_ref, gain_ref, s_ref, mine_ref, other_ref, attn_ref
):
    length = q_ref.shape[0]
    half = HD // 2
    lane = lax.broadcasted_iota(jnp.int32, (part, HD), 1)
    upper = half_ref[0] == 1
    for pair in range(s_ref.shape[0] // 2):
        packed = slice(pair * HD, (pair + 1) * HD)
        for first in range(0, length, part):
            last = first + part
            outs = []
            for head in (2 * pair, 2 * pair + 1):
                cols = slice(head * HD, (head + 1) * HD)
                queries = q_ref[first:last, cols]
                scores = masked(dot(queries, k_ref[:last, cols], NT), first)
                attn = dot(scores, v_ref[:last, cols], NN) + dot(queries, s_ref[head], NN)
                inv = lax.rsqrt(jnp.mean(attn * attn, axis=-1, keepdims=True) + 1e-06)
                outs.append(attn * inv * gain_ref[:, cols] * sigmoid(g_ref[first:last, cols]))
                attn_ref[first:last, cols] = attn
            low = jnp.where(lane < half, outs[0], pltpu.roll(outs[1], half, 1))
            high = jnp.where(lane < half, pltpu.roll(outs[0], half, 1), outs[1])
            mine_ref[first:last, packed] = jnp.where(upper, high, low).astype(BF16)
            other_ref[first:last, packed] = jnp.where(upper, low, high).astype(BF16)


def head_outputs(half, queries, keys, values, gate, gain, state, deps):
    length, inner = queries.shape
    heads = inner // HD
    step = 4
    rows = pl.BlockSpec((length, step * HD), lambda i: (0, i))
    packed_rows = pl.BlockSpec((length, step * HD // 2), lambda i: (0, i))
    square = pl.BlockSpec((step, HD, HD), lambda i: (i, 0, 0))
    packed = jax.ShapeDtypeStruct((length, inner // 2), BF16)
    in_specs = [
        pl.BlockSpec(memory_space=pltpu.SMEM),
        rows,
        rows,
        rows,
        rows,
        pl.BlockSpec((1, step * HD), lambda i: (0, i)),
        square,
    ]
    operands = [half, queries, keys, values, gate, gain, state]
    kernel = functools.partial(head_out_kernel, 256)
    kernel, operands, in_specs = tied(kernel, operands, in_specs, deps)
    return pl.pallas_call(
        kernel,
        grid=(heads // step,),
        in_specs=in_specs,
        out_specs=[packed_rows, packed_rows, rows],
        out_shape=[packed, packed, jax.ShapeDtypeStruct((length, inner), F32)],
        compiler_params=params(),
        cost_estimate=cost(4 * length * length * inner, 14 * length * inner),
    )(*operands)


def head_back_kernel(
    q_ref, g_ref, gain_ref, attn_ref, own_ref, far_ref, gate_ref, hi_ref, lo_ref, state_ref
):
    for head in range(state_ref.shape[0]):
        cols = slice(head * HD, (head + 1) * HD)
        gain = gain_ref[:, cols]
        attn = attn_ref[:, cols]
        inv = lax.rsqrt(jnp.mean(attn * attn, axis=-1, keepdims=True) + 1e-06)
        sig = sigmoid(g_ref[:, cols])
        grad = own_ref[:, cols] + far_ref[:, cols].astype(F32)
        unit = attn * inv
        scaled = grad * sig * gain
        product = scaled * unit
        gate_ref[:, cols] = (product * (1.0 - sig)).astype(BF16)
        full = inv * (scaled - unit * jnp.mean(product, axis=-1, keepdims=True))
        high = full.astype(BF16)
        hi_ref[:, cols] = high
        lo_ref[:, cols] = (full - high.astype(F32)).astype(BF16)
        state_ref[head] = dot(q_ref[:, cols], high, TN)


def head_back(queries, gate, gain, attn, own, far):
    length, inner = queries.shape
    heads = inner // HD
    step = 4
    rows = pl.BlockSpec((length, step * HD), lambda i: (0, i))
    square = pl.BlockSpec((step, HD, HD), lambda i: (i, 0, 0))
    wide = jax.ShapeDtypeStruct((length, inner), BF16)
    return pl.pallas_call(
        head_back_kernel,
        grid=(heads // step,),
        in_specs=[rows, rows, pl.BlockSpec((1, step * HD), lambda i: (0, i)), rows, rows, rows],
        out_specs=[rows, rows, rows, square],
        out_shape=[wide, wide, wide, jax.ShapeDtypeStruct((heads, HD, HD), F32)],
        compiler_params=params(),
        cost_estimate=cost(2 * length * HD * inner, 20 * length * inner),
    )(queries, gate, gain, attn, own, far)


def grads_kernel(
    part, q_ref, k_ref, v_ref, hi_ref, lo_ref, s_ref, dq_ref, dk_ref, dv_ref
):
    length = q_ref.shape[0]
    for head in range(s_ref.shape[0]):
        cols = slice(head * HD, (head + 1) * HD)
        for first in range(0, length, part):
            last = first + part
            queries, high = q_ref[first:last, cols], hi_ref[first:last, cols]
            keys, values = k_ref[:last, cols], v_ref[:last, cols]
            scores = masked(dot(queries, keys, NT), first)
            prob = dot(high, values, NT) + dot(lo_ref[first:last, cols], values, NT)
            prob = masked(prob, first)
            dq = dot(prob, keys, NN) + dot(high, s_ref[head], NT)
            dq_ref[first:last, cols] = dq.astype(BF16)
            dk = dot(prob, queries, TN)
            dv = dot(scores, high, TN)
            if first:
                dk_ref[:first, cols] += dk[:first]
                dv_ref[:first, cols] += dv[:first]
            dk_ref[first:last, cols] = dk[first:]
            dv_ref[first:last, cols] = dv[first:]


def head_grads(queries, keys, values, high, low, state, deps):
    length, inner = queries.shape
    heads = inner // HD
    step = 2
    rows = pl.BlockSpec((length, step * HD), lambda i: (0, i))
    square = pl.BlockSpec((step, HD, HD), lambda i: (i, 0, 0))
    wide = jax.ShapeDtypeStruct((length, inner), BF16)
    full = jax.ShapeDtypeStruct((length, inner), F32)
    kernel = functools.partial(grads_kernel, 256)
    operands = [queries, keys, values, high, low, state]
    kernel, operands, in_specs = tied(
        kernel, operands, [rows, rows, rows, rows, rows, square], deps
    )
    return pl.pallas_call(
        kernel,
        grid=(heads // step,),
        in_specs=in_specs,
        out_specs=[rows, rows, rows],
        out_shape=[wide, full, full],
        compiler_params=params(),
        cost_estimate=cost(10 * length * length * inner, 20 * length * inner),
    )(*operands)


def later_kernel(k_ref, v_ref, dk_ref, dv_ref, l_ref, dk_out, dv_out):
    groups = HD // (2 * l_ref.shape[1])
    for head in range(l_ref.shape[0] // 2):
        cols = slice(head * HD, (head + 1) * HD)
        later = jnp.concatenate(
            [
                l_ref[2 * head + piece, :, group * HD : (group + 1) * HD]
                for piece in range(2)
                for group in range(groups)
            ],
            axis=0,
        )
        dk_out[:, cols] = (dk_ref[:, cols] + dot(v_ref[:, cols], later, NT)).astype(BF16)
        dv_out[:, cols] = (dv_ref[:, cols] + dot(k_ref[:, cols], later, NN)).astype(BF16)


def later_grads(keys, values, key_part, value_part, parts, deps):
    length, inner = keys.shape
    heads = inner // HD
    step = 4
    rows = pl.BlockSpec((length, step * HD), lambda i: (0, i))
    wide = jax.ShapeDtypeStruct((length, inner), BF16)
    last = parts.shape[1] // 16 - 1
    in_specs = [
        rows,
        rows,
        rows,
        rows,
        pl.BlockSpec((2 * step, 16, parts.shape[2]), lambda i: (i, last, 0)),
    ]
    operands = [keys, values, key_part, value_part, parts]
    kernel, operands, in_specs = tied(later_kernel, operands, in_specs, deps)
    return pl.pallas_call(
        kernel,
        grid=(heads // step,),
        in_specs=in_specs,
        out_specs=[rows, rows],
        out_shape=[wide, wide],
        compiler_params=params(),
        cost_estimate=cost(4 * length * HD * inner, 16 * length * inner),
    )(*operands)


def mixed_kernel(sel_ref, *refs):
    blocks, w_ref, o_ref = refs[:-2], refs[-2], refs[-1]
    half = HD // 2
    total = None
    for place, block in enumerate(blocks):
        rows = []
        for head in range(block.shape[1] // half):
            first = sel_ref[2 * place] * 1024 + sel_ref[2 * place + 1] * half + head * HD
            rows.append(w_ref[pl.ds(pl.multiple_of(first, half), half), :])
        term = dot(block[...], jnp.concatenate(rows, axis=0), NN)
        total = term if total is None else total + term
    o_ref[...] = total.astype(BF16)


def mix(sel, blocks, w_out, deps):
    length, width = blocks[0].shape
    inner, features = w_out.shape
    tile = 256
    whole = pl.BlockSpec((length, width), lambda j, s: (0, 0))
    in_specs = [whole] * len(blocks) + [pl.BlockSpec((inner, tile), lambda j, s: (0, j))]
    kernel, operands, in_specs = tied(mixed_kernel, [sel, *blocks, w_out], in_specs, deps)
    return pl.pallas_call(
        kernel,
        grid_spec=pltpu.PrefetchScalarGridSpec(
            num_scalar_prefetch=1,
            grid=(features // tile,),
            in_specs=in_specs,
            out_specs=pl.BlockSpec((length, tile), lambda j, s: (0, j)),
        ),
        out_shape=jax.ShapeDtypeStruct((length, features), BF16),
        compiler_params=params(),
        cost_estimate=cost(2 * length * inner * features, 2 * inner * features),
    )(*operands)


def weight_kernel(sel_ref, a0_ref, a1_ref, b0_ref, b1_ref, m0_ref, m1_ref, *rest):
    o_ref = rest[-1]
    count, size = o_ref.shape[:2]
    for source, (first, second) in enumerate(((a0_ref, a1_ref), (b0_ref, b1_ref))):

        @pl.when(pl.program_id(0) == source)
        def _(first=first, second=second):
            total = dot(first[...], m0_ref[...], TN) + dot(second[...], m1_ref[...], TN)
            for piece in range(count):
                o_ref[piece] = total[piece * size : (piece + 1) * size].astype(BF16)


def weight_grad(sel, mine, other, grads, across, index, target=None, deps=()):
    length, width = mine[0].shape
    features = grads[0].shape[1]
    size = 2 * width // across
    tile = 512
    tiles, count = width // tile, tile // size
    last = tiles - 1

    def place(i, j, s):
        return ((s[0] + i - 2 * s[0] * i) * tiles + j, index, 0)

    first_rows = pl.BlockSpec((length, tile), lambda i, j, s: (0, jnp.where(i == 0, j, last)))
    second_rows = pl.BlockSpec((length, tile), lambda i, j, s: (0, jnp.where(i == 0, 0, j)))
    whole = pl.BlockSpec((length, features), lambda i, j, s: (0, 0))
    in_specs = [first_rows, first_rows, second_rows, second_rows, whole, whole]
    operands = [sel, mine[0], mine[1], other[0], other[1], *grads]
    aliases = {}
    if target is not None:
        in_specs.append(pl.BlockSpec(memory_space=pl.ANY))
        operands.append(target)
        aliases = {len(operands) - 1: 0}
    kernel, operands, in_specs = tied(weight_kernel, operands, in_specs, deps)
    return pl.pallas_call(
        kernel,
        grid_spec=pltpu.PrefetchScalarGridSpec(
            num_scalar_prefetch=1,
            grid=(2, tiles),
            in_specs=in_specs,
            out_specs=pl.BlockSpec((count, size, features), place),
        ),
        out_shape=jax.ShapeDtypeStruct((across, 2 * size + 16, features), BF16),
        input_output_aliases=aliases,
        compiler_params=params(),
        cost_estimate=cost(8 * length * width * features, 4 * width * features),
    )(*operands)


def per_device(query_rows, key_rows, value_rows, gate_input, norm_gain, w_out, mixed_grad):
    length, inner_dev = query_rows.shape
    heads_dev = inner_dev // HD
    features = w_out.shape[1]
    planes, across = 2, 16
    ctx, fsdp = lax.axis_index("ctx"), lax.axis_index("fsdp")
    y_lo = ctx // across
    y_hi, core = fsdp // 2, fsdp % 2
    groups = [[y * across + i for i in range(across)] for y in range(planes)]
    core_swap = [(0, 1), (1, 0), (2, 3), (3, 2)]
    hi_swap = [(0, 2), (1, 3), (2, 0), (3, 1)]
    lo_swap = [(i, (i + across) % (2 * across)) for i in range(2 * across)]

    def swap_core(array):
        return lax.ppermute(array, "fsdp", core_swap)

    def swap_hi(array):
        return lax.ppermute(array, "fsdp", hi_swap)

    def swap_lo(array):
        return lax.ppermute(array, "ctx", lo_swap)

    def exchange(array):
        return lax.all_to_all(array, "ctx", 0, 0, axis_index_groups=groups)

    def sums_before(pieces, offset, reverse, target=None, deps=()):
        use = (y_lo == (0 if reverse else 1)).astype(jnp.int32).reshape(1)
        return running_sum(pieces, offset, use, reverse, target, deps)

    def split_states(local):
        return exchange(local.reshape(across, heads_dev * HD // across, HD))

    gain = norm_gain.reshape(1, inner_dev)
    peer, far = fsdp + 1 - 2 * core, (fsdp + 2) % 4
    far_peer = (peer + 2) % 4

    def term(place, dtype, received=None, deps=()):
        return head_term(place, mixed_grad, w_out, inner_dev, dtype, received, deps)

    def term(places, dtype, received=None, part=0):
        return head_term(places, mixed_grad, w_out, inner_dev, dtype, received, part)

    grad_pair = swap_lo(mixed_grad)
    sent = term([far_peer, peer], BF16)
    got = swap_core(sent)
    local_state = block_states(after(key_rows, sent), value_rows)
    pieces = split_states(local_state)
    total = jnp.sum(pieces, axis=0)
    offset = swap_lo(total)
    far_part = term([after(far, total)], BF16, got, 0)[0]
    grad_far = swap_hi(after(far_part, offset, grad_pair))
    sums = sums_before(after(pieces, far_part), offset, False)
    grad_own = term([after(fsdp, sums)], F32, got, 1)[0]
    prev_state = exchange(sums).reshape(heads_dev, HD, HD)

    half = y_lo.astype(jnp.int32).reshape(1)
    out, out_other, attn = head_outputs(
        half, after(query_rows, grad_own), key_rows, value_rows, gate_input, gain, prev_state, []
    )
    gate_grad, high, low, grad_state = head_back(
        query_rows, gate_input, gain, attn, grad_own, grad_far
    )
    later_pieces = split_states(grad_state)
    later_total = jnp.sum(later_pieces, axis=0)

    across_y = []
    for place in range(2 * across):
        for part in range(4):
            target = ((place + across) % (2 * across)) * 4 + (part + 2) % 4
            across_y.append((place * 4 + part, target))
    out_pair = swap_lo(out_other)
    out_far = swap_hi(out)
    out_far_pair = lax.ppermute(out_other, ("ctx", "fsdp"), across_y)
    out_core, out_pair_core = (
        swap_core(after(out, grad_state)), swap_core(after(out_pair, grad_state))
    )
    out_far_core, out_far_pair_core = swap_core(out_far), swap_core(out_far_pair)
    select = core.astype(jnp.int32).reshape(1)
    grads = [mixed_grad, grad_pair]
    weight = weight_grad(
        select, [out, out_pair], [out_core, out_pair_core], grads, across, 0, deps=[grad_state]
    )
    weight = weight_grad(
        select, [out_far, out_far_pair], [out_far_core, out_far_pair_core], grads, across, 1,
        weight,
    )
    later_offset = swap_lo(later_total)
    weight = sums_before(later_pieces, later_offset, True, weight)
    parts = exchange(weight)
    far_other = swap_hi(out_other)
    query_grad, key_part, value_part = head_grads(
        query_rows, key_rows, value_rows, high, low, prev_state, [weight]
    )

    blocks = [out, out_other, out_core, swap_core(out_other)]
    blocks += [out_far, far_other, out_far_core, swap_core(far_other)]
    order = []
    for heads in (fsdp, peer, far, far_peer):
        order += [heads, y_lo, heads, 1 - y_lo]
    order = jnp.stack(order).astype(jnp.int32)
    mixed = mix(order, blocks, w_out, [query_grad])

    parts = after(parts, mixed)
    key_grad, value_grad = later_grads(key_rows, value_rows, key_part, value_part, parts, [])
    size = 2 * inner_dev // (2 * across)
    near_sum = jnp.sum(parts[:, :size].astype(F32), axis=0)
    far_sum = jnp.sum(parts[:, size : 2 * size].astype(F32), axis=0)
    keeps = y_hi == y_lo
    kept = jnp.where(keeps, near_sum, far_sum)
    received = swap_lo(jnp.where(keeps, far_sum, near_sum))
    w_out_grad = jnp.where(
        y_lo == 0,
        jnp.concatenate([kept, received], axis=0),
        jnp.concatenate([received, kept], axis=0),
    )
    return (mixed, w_out_grad, query_grad, key_grad, value_grad, gate_grad)


def solution(mesh):
    return jax.shard_map(
        per_device,
        mesh=mesh,
        in_specs=(
            P("ctx", "fsdp"),
            P("ctx", "fsdp"),
            P("ctx", "fsdp"),
            P("ctx", "fsdp"),
            P("fsdp"),
            P(None, "fsdp"),
            P("ctx", "fsdp"),
        ),
        out_specs=(
            P("ctx", "fsdp"),
            P("ctx", "fsdp"),
            P("ctx", "fsdp"),
            P("ctx", "fsdp"),
            P("ctx", "fsdp"),
            P("ctx", "fsdp"),
        ),
        check_vma=False,
    )
```

```python
import functools

import jax
import jax.numpy as jnp
from jax import lax
from jax.experimental import pallas as pl
from jax.experimental.pallas import tpu as pltpu
from jax.sharding import PartitionSpec as P

HD = 128
F32 = jnp.float32
BF16 = jnp.bfloat16
VMEM_LIMIT = 52 * 1024 * 1024

NT = (((1,), (1,)), ((), ()))
TN = (((0,), (0,)), ((), ()))
NN = (((1,), (0,)), ((), ()))


def dot(a, b, dims):
    return lax.dot_general(a, b, dims, preferred_element_type=F32)


def after(array, *others):
    return lax.optimization_barrier((array,) + others)[0]


def tied(kernel, operands, in_specs, deps):
    count = len(operands)

    def run(*refs):
        kernel(*refs[:count], *refs[count + len(deps) :])

    specs = [pl.BlockSpec(memory_space=pl.ANY)] * len(deps)
    return run, list(operands) + list(deps), list(in_specs) + specs


def params():
    return pltpu.CompilerParams(vmem_limit_bytes=VMEM_LIMIT)


def cost(flops, nbytes):
    return pl.CostEstimate(flops=flops, bytes_accessed=nbytes, transcendentals=0)


def state_kernel(k_ref, v_ref, s_ref):
    for head in range(s_ref.shape[0]):
        cols = slice(head * HD, (head + 1) * HD)
        s_ref[head] = dot(k_ref[:, cols], v_ref[:, cols], TN)


def block_states(keys, values):
    length, inner = keys.shape
    heads = inner // HD
    step = 4
    rows = pl.BlockSpec((length, step * HD), lambda i: (0, i))
    return pl.pallas_call(
        state_kernel,
        grid=(heads // step,),
        in_specs=[rows, rows],
        out_specs=pl.BlockSpec((step, HD, HD), lambda i: (i, 0, 0)),
        out_shape=jax.ShapeDtypeStruct((heads, HD, HD), F32),
        compiler_params=params(),
        cost_estimate=cost(2 * length * inner * HD, 4 * length * inner),
    )(keys, values)


def running_kernel(reverse, count, use_ref, p_ref, offset_ref, *rest):
    out_ref = rest[-1]
    rows, lanes = out_ref.shape[1], p_ref.shape[2]
    groups = p_ref.shape[1] // rows
    if out_ref.shape[2] > groups * lanes:
        out_ref[...] = jnp.zeros(out_ref.shape, out_ref.dtype)
    total = offset_ref[...] * use_ref[0].astype(F32)
    for step in range(count):
        place = count - 1 - step if reverse else step
        piece = total.astype(out_ref.dtype)
        for group in range(groups):
            cols = slice(group * lanes, (group + 1) * lanes)
            out_ref[place, :, cols] = piece[group * rows : (group + 1) * rows]
        if step < count - 1:
            total = total + p_ref[place]


def running_sum(pieces, offset, use, reverse, target=None, deps=()):
    count, rows, lanes = pieces.shape
    in_specs = [
        pl.BlockSpec(memory_space=pltpu.SMEM),
        pl.BlockSpec(pieces.shape, lambda i: (0, 0, 0)),
        pl.BlockSpec(offset.shape, lambda i: (0, 0)),
    ]
    operands = [use, pieces, offset]
    if target is None:
        aliases = {}
        out_spec = pl.BlockSpec(pieces.shape, lambda i: (0, 0, 0))
        out_shape = jax.ShapeDtypeStruct(pieces.shape, BF16)
    else:
        aliases = {3: 0}
        in_specs.append(pl.BlockSpec(memory_space=pl.ANY))
        operands.append(target)
        last = target.shape[1] // 16 - 1
        out_spec = pl.BlockSpec((count, 16, target.shape[2]), lambda i: (0, last, 0))
        out_shape = jax.ShapeDtypeStruct(target.shape, BF16)
    kernel = functools.partial(running_kernel, reverse, count)
    kernel, operands, in_specs = tied(kernel, operands, in_specs, deps)
    return pl.pallas_call(
        kernel,
        grid=(1,),
        in_specs=in_specs,
        out_specs=out_spec,
        out_shape=out_shape,
        input_output_aliases=aliases,
        compiler_params=params(),
        cost_estimate=cost(count * rows * lanes, 6 * count * rows * lanes),
    )(*operands)


def head_term_kernel(sel_ref, a_ref, w_ref, o_ref):
    o_ref[0] = dot(a_ref[...], w_ref[...], NT).astype(o_ref.dtype)


def head_sum_kernel(sel_ref, a_ref, w_ref, r_ref, o_ref):
    total = dot(a_ref[...], w_ref[...], NT) + r_ref[0].astype(F32)
    o_ref[0] = total.astype(o_ref.dtype)


def head_term(places, grad, w_out, width, dtype, received=None, part=0):
    length, features = grad.shape
    count = len(places)
    tile = 512 if count == 1 else width
    tiles = width // tile
    in_specs = [
        pl.BlockSpec((length, features), lambda i, j, s: (0, 0)),
        pl.BlockSpec((tile, features), lambda i, j, s: (s[i] * tiles + j, 0)),
    ]
    operands = [jnp.stack(places).astype(jnp.int32), grad, w_out]
    if received is not None:
        in_specs.append(pl.BlockSpec((1, length, tile), lambda i, j, s: (part, 0, j)))
        operands.append(received)
    return pl.pallas_call(
        head_term_kernel if received is None else head_sum_kernel,
        grid_spec=pltpu.PrefetchScalarGridSpec(
            num_scalar_prefetch=1,
            grid=(count, tiles),
            in_specs=in_specs,
            out_specs=pl.BlockSpec((1, length, tile), lambda i, j, s: (i, 0, j)),
        ),
        out_shape=jax.ShapeDtypeStruct((count, length, width), dtype),
        compiler_params=params(),
        cost_estimate=cost(2 * length * features * width, 4 * width * features),
    )(*operands)


def score_rows(q_ref, k_ref, first, size):
    last = first + size
    scores = dot(q_ref[first:last], k_ref[:last], NT)
    return masked(scores, first)


def masked(scores, first):
    rows = lax.broadcasted_iota(jnp.int32, scores.shape, 0) + first
    cols = lax.broadcasted_iota(jnp.int32, scores.shape, 1)
    return jnp.where(cols <= rows, scores, 0.0).astype(BF16)


def sigmoid(gate):
    return 0.5 * jnp.tanh(0.5 * gate.astype(F32)) + 0.5


def head_out_kernel(
    part, half_ref, q_ref, k_ref, v_ref, g_ref, gain_ref, s_ref, mine_ref, other_ref, attn_ref
):
    length = q_ref.shape[0]
    half = HD // 2
    lane = lax.broadcasted_iota(jnp.int32, (part, HD), 1)
    upper = half_ref[0] == 1
    for pair in range(s_ref.shape[0] // 2):
        packed = slice(pair * HD, (pair + 1) * HD)
        for first in range(0, length, part):
            last = first + part
            outs = []
            for head in (2 * pair, 2 * pair + 1):
                cols = slice(head * HD, (head + 1) * HD)
                queries = q_ref[first:last, cols]
                scores = masked(dot(queries, k_ref[:last, cols], NT), first)
                attn = dot(scores, v_ref[:last, cols], NN) + dot(queries, s_ref[head], NN)
                inv = lax.rsqrt(jnp.mean(attn * attn, axis=-1, keepdims=True) + 1e-06)
                outs.append(attn * inv * gain_ref[:, cols] * sigmoid(g_ref[first:last, cols]))
                attn_ref[first:last, cols] = attn
            low = jnp.where(lane < half, outs[0], pltpu.roll(outs[1], half, 1))
            high = jnp.where(lane < half, pltpu.roll(outs[0], half, 1), outs[1])
            mine_ref[first:last, packed] = jnp.where(upper, high, low).astype(BF16)
            other_ref[first:last, packed] = jnp.where(upper, low, high).astype(BF16)


def head_outputs(half, queries, keys, values, gate, gain, state, deps):
    length, inner = queries.shape
    heads = inner // HD
    step = 4
    rows = pl.BlockSpec((length, step * HD), lambda i: (0, i))
    packed_rows = pl.BlockSpec((length, step * HD // 2), lambda i: (0, i))
    square = pl.BlockSpec((step, HD, HD), lambda i: (i, 0, 0))
    packed = jax.ShapeDtypeStruct((length, inner // 2), BF16)
    in_specs = [
        pl.BlockSpec(memory_space=pltpu.SMEM),
        rows,
        rows,
        rows,
        rows,
        pl.BlockSpec((1, step * HD), lambda i: (0, i)),
        square,
    ]
    operands = [half, queries, keys, values, gate, gain, state]
    kernel = functools.partial(head_out_kernel, 256)
    kernel, operands, in_specs = tied(kernel, operands, in_specs, deps)
    return pl.pallas_call(
        kernel,
        grid=(heads // step,),
        in_specs=in_specs,
        out_specs=[packed_rows, packed_rows, rows],
        out_shape=[packed, packed, jax.ShapeDtypeStruct((length, inner), F32)],
        compiler_params=params(),
        cost_estimate=cost(4 * length * length * inner, 14 * length * inner),
    )(*operands)


def head_back_kernel(
    q_ref, g_ref, gain_ref, attn_ref, own_ref, far_ref, gate_ref, hi_ref, lo_ref, state_ref
):
    for head in range(state_ref.shape[0]):
        cols = slice(head * HD, (head + 1) * HD)
        gain = gain_ref[:, cols]
        attn = attn_ref[:, cols]
        inv = lax.rsqrt(jnp.mean(attn * attn, axis=-1, keepdims=True) + 1e-06)
        sig = sigmoid(g_ref[:, cols])
        grad = own_ref[:, cols] + far_ref[:, cols].astype(F32)
        unit = attn * inv
        scaled = grad * sig * gain
        product = scaled * unit
        gate_ref[:, cols] = (product * (1.0 - sig)).astype(BF16)
        full = inv * (scaled - unit * jnp.mean(product, axis=-1, keepdims=True))
        high = full.astype(BF16)
        hi_ref[:, cols] = high
        lo_ref[:, cols] = (full - high.astype(F32)).astype(BF16)
        state_ref[head] = dot(q_ref[:, cols], high, TN)


def head_back(queries, gate, gain, attn, own, far):
    length, inner = queries.shape
    heads = inner // HD
    step = 4
    rows = pl.BlockSpec((length, step * HD), lambda i: (0, i))
    square = pl.BlockSpec((step, HD, HD), lambda i: (i, 0, 0))
    wide = jax.ShapeDtypeStruct((length, inner), BF16)
    return pl.pallas_call(
        head_back_kernel,
        grid=(heads // step,),
        in_specs=[rows, rows, pl.BlockSpec((1, step * HD), lambda i: (0, i)), rows, rows, rows],
        out_specs=[rows, rows, rows, square],
        out_shape=[wide, wide, wide, jax.ShapeDtypeStruct((heads, HD, HD), F32)],
        compiler_params=params(),
        cost_estimate=cost(2 * length * HD * inner, 20 * length * inner),
    )(queries, gate, gain, attn, own, far)


def grads_kernel(
    part, q_ref, k_ref, v_ref, hi_ref, lo_ref, s_ref, dq_ref, dk_ref, dv_ref
):
    length = q_ref.shape[0]
    for head in range(s_ref.shape[0]):
        cols = slice(head * HD, (head + 1) * HD)
        for first in range(0, length, part):
            last = first + part
            queries, high = q_ref[first:last, cols], hi_ref[first:last, cols]
            keys, values = k_ref[:last, cols], v_ref[:last, cols]
            scores = masked(dot(queries, keys, NT), first)
            prob = dot(high, values, NT) + dot(lo_ref[first:last, cols], values, NT)
            prob = masked(prob, first)
            dq = dot(prob, keys, NN) + dot(high, s_ref[head], NT)
            dq_ref[first:last, cols] = dq.astype(BF16)
            dk = dot(prob, queries, TN)
            dv = dot(scores, high, TN)
            if first:
                dk_ref[:first, cols] += dk[:first]
                dv_ref[:first, cols] += dv[:first]
            dk_ref[first:last, cols] = dk[first:]
            dv_ref[first:last, cols] = dv[first:]


def head_grads(queries, keys, values, high, low, state, deps):
    length, inner = queries.shape
    heads = inner // HD
    step = 2
    rows = pl.BlockSpec((length, step * HD), lambda i: (0, i))
    square = pl.BlockSpec((step, HD, HD), lambda i: (i, 0, 0))
    wide = jax.ShapeDtypeStruct((length, inner), BF16)
    full = jax.ShapeDtypeStruct((length, inner), F32)
    kernel = functools.partial(grads_kernel, 256)
    operands = [queries, keys, values, high, low, state]
    kernel, operands, in_specs = tied(
        kernel, operands, [rows, rows, rows, rows, rows, square], deps
    )
    return pl.pallas_call(
        kernel,
        grid=(heads // step,),
        in_specs=in_specs,
        out_specs=[rows, rows, rows],
        out_shape=[wide, full, full],
        compiler_params=params(),
        cost_estimate=cost(10 * length * length * inner, 20 * length * inner),
    )(*operands)


def later_kernel(k_ref, v_ref, dk_ref, dv_ref, l_ref, dk_out, dv_out):
    groups = HD // (2 * l_ref.shape[1])
    for head in range(l_ref.shape[0] // 2):
        cols = slice(head * HD, (head + 1) * HD)
        later = jnp.concatenate(
            [
                l_ref[2 * head + piece, :, group * HD : (group + 1) * HD]
                for piece in range(2)
                for group in range(groups)
            ],
            axis=0,
        )
        dk_out[:, cols] = (dk_ref[:, cols] + dot(v_ref[:, cols], later, NT)).astype(BF16)
        dv_out[:, cols] = (dv_ref[:, cols] + dot(k_ref[:, cols], later, NN)).astype(BF16)


def later_grads(keys, values, key_part, value_part, parts, deps):
    length, inner = keys.shape
    heads = inner // HD
    step = 4
    rows = pl.BlockSpec((length, step * HD), lambda i: (0, i))
    wide = jax.ShapeDtypeStruct((length, inner), BF16)
    last = parts.shape[1] // 16 - 1
    in_specs = [
        rows,
        rows,
        rows,
        rows,
        pl.BlockSpec((2 * step, 16, parts.shape[2]), lambda i: (i, last, 0)),
    ]
    operands = [keys, values, key_part, value_part, parts]
    kernel, operands, in_specs = tied(later_kernel, operands, in_specs, deps)
    return pl.pallas_call(
        kernel,
        grid=(heads // step,),
        in_specs=in_specs,
        out_specs=[rows, rows],
        out_shape=[wide, wide],
        compiler_params=params(),
        cost_estimate=cost(4 * length * HD * inner, 16 * length * inner),
    )(*operands)


def mixed_kernel(sel_ref, *refs):
    blocks, w_ref, o_ref = refs[:-2], refs[-2], refs[-1]
    half = HD // 2
    total = None
    for place, block in enumerate(blocks):
        rows = []
        for head in range(block.shape[1] // half):
            first = sel_ref[2 * place] * 1024 + sel_ref[2 * place + 1] * half + head * HD
            rows.append(w_ref[pl.ds(pl.multiple_of(first, half), half), :])
        term = dot(block[...], jnp.concatenate(rows, axis=0), NN)
        total = term if total is None else total + term
    o_ref[...] = total.astype(BF16)


def mix(sel, blocks, w_out, deps):
    length, width = blocks[0].shape
    inner, features = w_out.shape
    tile = 256
    whole = pl.BlockSpec((length, width), lambda j, s: (0, 0))
    in_specs = [whole] * len(blocks) + [pl.BlockSpec((inner, tile), lambda j, s: (0, j))]
    kernel, operands, in_specs = tied(mixed_kernel, [sel, *blocks, w_out], in_specs, deps)
    return pl.pallas_call(
        kernel,
        grid_spec=pltpu.PrefetchScalarGridSpec(
            num_scalar_prefetch=1,
            grid=(features // tile,),
            in_specs=in_specs,
            out_specs=pl.BlockSpec((length, tile), lambda j, s: (0, j)),
        ),
        out_shape=jax.ShapeDtypeStruct((length, features), BF16),
        compiler_params=params(),
        cost_estimate=cost(2 * length * inner * features, 2 * inner * features),
    )(*operands)


def weight_kernel(sel_ref, a0_ref, a1_ref, b0_ref, b1_ref, m0_ref, m1_ref, *rest):
    o_ref = rest[-1]
    count, size = o_ref.shape[:2]
    for source, (first, second) in enumerate(((a0_ref, a1_ref), (b0_ref, b1_ref))):

        @pl.when(pl.program_id(0) == source)
        def _(first=first, second=second):
            total = dot(first[...], m0_ref[...], TN) + dot(second[...], m1_ref[...], TN)
            for piece in range(count):
                o_ref[piece] = total[piece * size : (piece + 1) * size].astype(BF16)


def weight_grad(sel, mine, other, grads, across, index, target=None, deps=()):
    length, width = mine[0].shape
    features = grads[0].shape[1]
    size = 2 * width // across
    tile = 512
    tiles, count = width // tile, tile // size
    last = tiles - 1

    def place(i, j, s):
        return ((s[0] + i - 2 * s[0] * i) * tiles + j, index, 0)

    first_rows = pl.BlockSpec((length, tile), lambda i, j, s: (0, jnp.where(i == 0, j, last)))
    second_rows = pl.BlockSpec((length, tile), lambda i, j, s: (0, jnp.where(i == 0, 0, j)))
    whole = pl.BlockSpec((length, features), lambda i, j, s: (0, 0))
    in_specs = [first_rows, first_rows, second_rows, second_rows, whole, whole]
    operands = [sel, mine[0], mine[1], other[0], other[1], *grads]
    aliases = {}
    if target is not None:
        in_specs.append(pl.BlockSpec(memory_space=pl.ANY))
        operands.append(target)
        aliases = {len(operands) - 1: 0}
    kernel, operands, in_specs = tied(weight_kernel, operands, in_specs, deps)
    return pl.pallas_call(
        kernel,
        grid_spec=pltpu.PrefetchScalarGridSpec(
            num_scalar_prefetch=1,
            grid=(2, tiles),
            in_specs=in_specs,
            out_specs=pl.BlockSpec((count, size, features), place),
        ),
        out_shape=jax.ShapeDtypeStruct((across, 2 * size + 16, features), BF16),
        input_output_aliases=aliases,
        compiler_params=params(),
        cost_estimate=cost(8 * length * width * features, 4 * width * features),
    )(*operands)


def per_device(query_rows, key_rows, value_rows, gate_input, norm_gain, w_out, mixed_grad):
    length, inner_dev = query_rows.shape
    heads_dev = inner_dev // HD
    features = w_out.shape[1]
    planes, across = 2, 16
    ctx, fsdp = lax.axis_index("ctx"), lax.axis_index("fsdp")
    y_lo = ctx // across
    y_hi, core = fsdp // 2, fsdp % 2
    groups = [[y * across + i for i in range(across)] for y in range(planes)]
    core_swap = [(0, 1), (1, 0), (2, 3), (3, 2)]
    hi_swap = [(0, 2), (1, 3), (2, 0), (3, 1)]
    lo_swap = [(i, (i + across) % (2 * across)) for i in range(2 * across)]

    def swap_core(array):
        return lax.ppermute(array, "fsdp", core_swap)

    def swap_hi(array):
        return lax.ppermute(array, "fsdp", hi_swap)

    def swap_lo(array):
        return lax.ppermute(array, "ctx", lo_swap)

    def exchange(array):
        return lax.all_to_all(array, "ctx", 0, 0, axis_index_groups=groups)

    def sums_before(pieces, offset, reverse, target=None, deps=()):
        use = (y_lo == (0 if reverse else 1)).astype(jnp.int32).reshape(1)
        return running_sum(pieces, offset, use, reverse, target, deps)

    def split_states(local):
        return exchange(local.reshape(across, heads_dev * HD // across, HD))

    gain = norm_gain.reshape(1, inner_dev)
    peer, far = fsdp + 1 - 2 * core, (fsdp + 2) % 4
    far_peer = (peer + 2) % 4

    def term(place, dtype, received=None, deps=()):
        return head_term(place, mixed_grad, w_out, inner_dev, dtype, received, deps)

    def term(places, dtype, received=None, part=0):
        return head_term(places, mixed_grad, w_out, inner_dev, dtype, received, part)

    grad_pair = swap_lo(mixed_grad)
    sent = term([far_peer, peer], BF16)
    got = swap_core(sent)
    local_state = block_states(after(key_rows, sent), value_rows)
    pieces = split_states(local_state)
    far_part = term([far], BF16, got, 0)[0]
    total = jnp.sum(after(pieces, far_part), axis=0)
    offset = swap_lo(total)
    grad_far = swap_hi(after(far_part, offset, grad_pair))
    sums = sums_before(after(pieces, far_part), offset, False)
    grad_own = term([after(fsdp, sums)], F32, got, 1)[0]
    prev_state = exchange(sums).reshape(heads_dev, HD, HD)

    half = y_lo.astype(jnp.int32).reshape(1)
    out, out_other, attn = head_outputs(
        half, after(query_rows, grad_own), key_rows, value_rows, gate_input, gain, prev_state, []
    )
    gate_grad, high, low, grad_state = head_back(
        query_rows, gate_input, gain, attn, grad_own, grad_far
    )
    later_pieces = split_states(grad_state)
    later_total = jnp.sum(later_pieces, axis=0)

    across_y = []
    for place in range(2 * across):
        for part in range(4):
            target = ((place + across) % (2 * across)) * 4 + (part + 2) % 4
            across_y.append((place * 4 + part, target))
    out_pair = swap_lo(out_other)
    out_far = swap_hi(out)
    out_far_pair = lax.ppermute(out_other, ("ctx", "fsdp"), across_y)
    out_core, out_pair_core = (
        swap_core(after(out, grad_state)), swap_core(after(out_pair, grad_state))
    )
    out_far_core, out_far_pair_core = swap_core(out_far), swap_core(out_far_pair)
    select = core.astype(jnp.int32).reshape(1)
    grads = [mixed_grad, grad_pair]
    weight = weight_grad(
        select, [out, out_pair], [out_core, out_pair_core], grads, across, 0, deps=[grad_state]
    )
    weight = weight_grad(
        select, [out_far, out_far_pair], [out_far_core, out_far_pair_core], grads, across, 1,
        weight,
    )
    later_offset = swap_lo(later_total)
    weight = sums_before(later_pieces, later_offset, True, weight)
    parts = exchange(weight)
    far_other = swap_hi(out_other)
    query_grad, key_part, value_part = head_grads(
        query_rows, key_rows, value_rows, high, low, prev_state, [weight]
    )

    blocks = [out, out_other, out_core, swap_core(out_other)]
    blocks += [out_far, far_other, out_far_core, swap_core(far_other)]
    order = []
    for heads in (fsdp, peer, far, far_peer):
        order += [heads, y_lo, heads, 1 - y_lo]
    order = jnp.stack(order).astype(jnp.int32)
    mixed = mix(order, blocks, w_out, [query_grad])

    parts = after(parts, mixed)
    key_grad, value_grad = later_grads(key_rows, value_rows, key_part, value_part, parts, [])
    size = 2 * inner_dev // (2 * across)
    near_sum = jnp.sum(parts[:, :size].astype(F32), axis=0)
    far_sum = jnp.sum(parts[:, size : 2 * size].astype(F32), axis=0)
    keeps = y_hi == y_lo
    kept = jnp.where(keeps, near_sum, far_sum)
    received = swap_lo(jnp.where(keeps, far_sum, near_sum))
    w_out_grad = jnp.where(
        y_lo == 0,
        jnp.concatenate([kept, received], axis=0),
        jnp.concatenate([received, kept], axis=0),
    )
    return (mixed, w_out_grad, query_grad, key_grad, value_grad, gate_grad)


def solution(mesh):
    return jax.shard_map(
        per_device,
        mesh=mesh,
        in_specs=(
            P("ctx", "fsdp"),
            P("ctx", "fsdp"),
            P("ctx", "fsdp"),
            P("ctx", "fsdp"),
            P("fsdp"),
            P(None, "fsdp"),
            P("ctx", "fsdp"),
        ),
        out_specs=(
            P("ctx", "fsdp"),
            P("ctx", "fsdp"),
            P("ctx", "fsdp"),
            P("ctx", "fsdp"),
            P("ctx", "fsdp"),
            P("ctx", "fsdp"),
        ),
        check_vma=False,
    )
```

```python
import functools

import jax
import jax.numpy as jnp
from jax import lax
from jax.experimental import pallas as pl
from jax.experimental.pallas import tpu as pltpu
from jax.sharding import PartitionSpec as P

HD = 128
F32 = jnp.float32
BF16 = jnp.bfloat16
VMEM_LIMIT = 44 * 1024 * 1024

NT = (((1,), (1,)), ((), ()))
TN = (((0,), (0,)), ((), ()))
NN = (((1,), (0,)), ((), ()))


def dot(a, b, dims):
    return lax.dot_general(a, b, dims, preferred_element_type=F32)


def after(array, *others):
    return lax.optimization_barrier((array,) + others)[0]


def tied(kernel, operands, in_specs, deps):
    count = len(operands)

    def run(*refs):
        kernel(*refs[:count], *refs[count + len(deps) :])

    specs = [pl.BlockSpec(memory_space=pl.ANY)] * len(deps)
    return run, list(operands) + list(deps), list(in_specs) + specs


def params():
    return pltpu.CompilerParams(vmem_limit_bytes=VMEM_LIMIT)


def cost(flops, nbytes):
    return pl.CostEstimate(flops=flops, bytes_accessed=nbytes, transcendentals=0)


def state_kernel(k_ref, v_ref, s_ref):
    for head in range(s_ref.shape[0]):
        cols = slice(head * HD, (head + 1) * HD)
        s_ref[head] = dot(k_ref[:, cols], v_ref[:, cols], TN)


def block_states(keys, values):
    length, inner = keys.shape
    heads = inner // HD
    step = 4
    rows = pl.BlockSpec((length, step * HD), lambda i: (0, i))
    return pl.pallas_call(
        state_kernel,
        grid=(heads // step,),
        in_specs=[rows, rows],
        out_specs=pl.BlockSpec((step, HD, HD), lambda i: (i, 0, 0)),
        out_shape=jax.ShapeDtypeStruct((heads, HD, HD), F32),
        compiler_params=params(),
        cost_estimate=cost(2 * length * inner * HD, 4 * length * inner),
    )(keys, values)


def running_kernel(reverse, count, use_ref, p_ref, offset_ref, *rest):
    out_ref = rest[-1]
    rows, lanes = out_ref.shape[1], p_ref.shape[2]
    groups = p_ref.shape[1] // rows
    if out_ref.shape[2] > groups * lanes:
        out_ref[...] = jnp.zeros(out_ref.shape, out_ref.dtype)
    total = offset_ref[...] * use_ref[0].astype(F32)
    for step in range(count):
        place = count - 1 - step if reverse else step
        piece = total.astype(out_ref.dtype)
        for group in range(groups):
            cols = slice(group * lanes, (group + 1) * lanes)
            out_ref[place, :, cols] = piece[group * rows : (group + 1) * rows]
        if step < count - 1:
            total = total + p_ref[place]


def running_sum(pieces, offset, use, reverse, target=None, deps=()):
    count, rows, lanes = pieces.shape
    in_specs = [
        pl.BlockSpec(memory_space=pltpu.SMEM),
        pl.BlockSpec(pieces.shape, lambda i: (0, 0, 0)),
        pl.BlockSpec(offset.shape, lambda i: (0, 0)),
    ]
    operands = [use, pieces, offset]
    if target is None:
        aliases = {}
        out_spec = pl.BlockSpec(pieces.shape, lambda i: (0, 0, 0))
        out_shape = jax.ShapeDtypeStruct(pieces.shape, BF16)
    else:
        aliases = {3: 0}
        in_specs.append(pl.BlockSpec(memory_space=pl.ANY))
        operands.append(target)
        last = target.shape[1] // 16 - 1
        out_spec = pl.BlockSpec((count, 16, target.shape[2]), lambda i: (0, last, 0))
        out_shape = jax.ShapeDtypeStruct(target.shape, BF16)
    kernel = functools.partial(running_kernel, reverse, count)
    kernel, operands, in_specs = tied(kernel, operands, in_specs, deps)
    return pl.pallas_call(
        kernel,
        grid=(1,),
        in_specs=in_specs,
        out_specs=out_spec,
        out_shape=out_shape,
        input_output_aliases=aliases,
        compiler_params=params(),
        cost_estimate=cost(count * rows * lanes, 6 * count * rows * lanes),
    )(*operands)


def head_term_kernel(sel_ref, a_ref, w_ref, o_ref):
    o_ref[0] = dot(a_ref[...], w_ref[...], NT).astype(o_ref.dtype)


def head_sum_kernel(sel_ref, a_ref, w_ref, r_ref, o_ref):
    total = dot(a_ref[...], w_ref[...], NT) + r_ref[0].astype(F32)
    o_ref[0] = total.astype(o_ref.dtype)


def head_term(places, grad, w_out, width, dtype, received=None, part=0):
    length, features = grad.shape
    count = len(places)
    tile = 512 if count == 1 else width
    tiles = width // tile
    in_specs = [
        pl.BlockSpec((length, features), lambda i, j, s: (0, 0)),
        pl.BlockSpec((tile, features), lambda i, j, s: (s[i] * tiles + j, 0)),
    ]
    operands = [jnp.stack(places).astype(jnp.int32), grad, w_out]
    if received is not None:
        in_specs.append(pl.BlockSpec((1, length, tile), lambda i, j, s: (part, 0, j)))
        operands.append(received)
    return pl.pallas_call(
        head_term_kernel if received is None else head_sum_kernel,
        grid_spec=pltpu.PrefetchScalarGridSpec(
            num_scalar_prefetch=1,
            grid=(count, tiles),
            in_specs=in_specs,
            out_specs=pl.BlockSpec((1, length, tile), lambda i, j, s: (i, 0, j)),
        ),
        out_shape=jax.ShapeDtypeStruct((count, length, width), dtype),
        compiler_params=params(),
        cost_estimate=cost(2 * length * features * width, 4 * width * features),
    )(*operands)


def score_rows(q_ref, k_ref, first, size):
    last = first + size
    scores = dot(q_ref[first:last], k_ref[:last], NT)
    return masked(scores, first)


def masked(scores, first):
    rows = lax.broadcasted_iota(jnp.int32, scores.shape, 0) + first
    cols = lax.broadcasted_iota(jnp.int32, scores.shape, 1)
    return jnp.where(cols <= rows, scores, 0.0).astype(BF16)


def sigmoid(gate):
    return 0.5 * jnp.tanh(0.5 * gate.astype(F32)) + 0.5


def head_out_kernel(
    part, half_ref, q_ref, k_ref, v_ref, g_ref, gain_ref, s_ref, mine_ref, other_ref, attn_ref
):
    length = q_ref.shape[0]
    half = HD // 2
    lane = lax.broadcasted_iota(jnp.int32, (part, HD), 1)
    upper = half_ref[0] == 1
    for pair in range(s_ref.shape[0] // 2):
        packed = slice(pair * HD, (pair + 1) * HD)
        for first in range(0, length, part):
            last = first + part
            outs = []
            for head in (2 * pair, 2 * pair + 1):
                cols = slice(head * HD, (head + 1) * HD)
                queries = q_ref[first:last, cols]
                scores = masked(dot(queries, k_ref[:last, cols], NT), first)
                attn = dot(scores, v_ref[:last, cols], NN) + dot(queries, s_ref[head], NN)
                inv = lax.rsqrt(jnp.mean(attn * attn, axis=-1, keepdims=True) + 1e-06)
                outs.append(attn * inv * gain_ref[:, cols] * sigmoid(g_ref[first:last, cols]))
                attn_ref[first:last, cols] = attn
            low = jnp.where(lane < half, outs[0], pltpu.roll(outs[1], half, 1))
            high = jnp.where(lane < half, pltpu.roll(outs[0], half, 1), outs[1])
            mine_ref[first:last, packed] = jnp.where(upper, high, low).astype(BF16)
            other_ref[first:last, packed] = jnp.where(upper, low, high).astype(BF16)


def head_outputs(half, queries, keys, values, gate, gain, state, deps):
    length, inner = queries.shape
    heads = inner // HD
    step = 4
    rows = pl.BlockSpec((length, step * HD), lambda i: (0, i))
    packed_rows = pl.BlockSpec((length, step * HD // 2), lambda i: (0, i))
    square = pl.BlockSpec((step, HD, HD), lambda i: (i, 0, 0))
    packed = jax.ShapeDtypeStruct((length, inner // 2), BF16)
    in_specs = [
        pl.BlockSpec(memory_space=pltpu.SMEM),
        rows,
        rows,
        rows,
        rows,
        pl.BlockSpec((1, step * HD), lambda i: (0, i)),
        square,
    ]
    operands = [half, queries, keys, values, gate, gain, state]
    kernel = functools.partial(head_out_kernel, 256)
    kernel, operands, in_specs = tied(kernel, operands, in_specs, deps)
    return pl.pallas_call(
        kernel,
        grid=(heads // step,),
        in_specs=in_specs,
        out_specs=[packed_rows, packed_rows, rows],
        out_shape=[packed, packed, jax.ShapeDtypeStruct((length, inner), F32)],
        compiler_params=params(),
        cost_estimate=cost(4 * length * length * inner, 14 * length * inner),
    )(*operands)


def head_back_kernel(
    q_ref, g_ref, gain_ref, attn_ref, own_ref, far_ref, gate_ref, hi_ref, lo_ref, state_ref
):
    for head in range(state_ref.shape[0]):
        cols = slice(head * HD, (head + 1) * HD)
        gain = gain_ref[:, cols]
        attn = attn_ref[:, cols]
        inv = lax.rsqrt(jnp.mean(attn * attn, axis=-1, keepdims=True) + 1e-06)
        sig = sigmoid(g_ref[:, cols])
        grad = own_ref[:, cols] + far_ref[:, cols].astype(F32)
        unit = attn * inv
        scaled = grad * sig * gain
        product = scaled * unit
        gate_ref[:, cols] = (product * (1.0 - sig)).astype(BF16)
        full = inv * (scaled - unit * jnp.mean(product, axis=-1, keepdims=True))
        high = full.astype(BF16)
        hi_ref[:, cols] = high
        lo_ref[:, cols] = (full - high.astype(F32)).astype(BF16)
        state_ref[head] = dot(q_ref[:, cols], high, TN)


def head_back(queries, gate, gain, attn, own, far):
    length, inner = queries.shape
    heads = inner // HD
    step = 4
    rows = pl.BlockSpec((length, step * HD), lambda i: (0, i))
    square = pl.BlockSpec((step, HD, HD), lambda i: (i, 0, 0))
    wide = jax.ShapeDtypeStruct((length, inner), BF16)
    return pl.pallas_call(
        head_back_kernel,
        grid=(heads // step,),
        in_specs=[rows, rows, pl.BlockSpec((1, step * HD), lambda i: (0, i)), rows, rows, rows],
        out_specs=[rows, rows, rows, square],
        out_shape=[wide, wide, wide, jax.ShapeDtypeStruct((heads, HD, HD), F32)],
        compiler_params=params(),
        cost_estimate=cost(2 * length * HD * inner, 20 * length * inner),
    )(queries, gate, gain, attn, own, far)


def grads_kernel(
    part, q_ref, k_ref, v_ref, hi_ref, lo_ref, s_ref, dq_ref, dk_ref, dv_ref
):
    length = q_ref.shape[0]
    for head in range(s_ref.shape[0]):
        cols = slice(head * HD, (head + 1) * HD)
        for first in range(0, length, part):
            last = first + part
            queries, high = q_ref[first:last, cols], hi_ref[first:last, cols]
            keys, values = k_ref[:last, cols], v_ref[:last, cols]
            scores = masked(dot(queries, keys, NT), first)
            prob = dot(high, values, NT) + dot(lo_ref[first:last, cols], values, NT)
            prob = masked(prob, first)
            dq = dot(prob, keys, NN) + dot(high, s_ref[head], NT)
            dq_ref[first:last, cols] = dq.astype(BF16)
            dk = dot(prob, queries, TN)
            dv = dot(scores, high, TN)
            if first:
                dk_ref[:first, cols] += dk[:first]
                dv_ref[:first, cols] += dv[:first]
            dk_ref[first:last, cols] = dk[first:]
            dv_ref[first:last, cols] = dv[first:]


def head_grads(queries, keys, values, high, low, state, deps):
    length, inner = queries.shape
    heads = inner // HD
    step = 2
    rows = pl.BlockSpec((length, step * HD), lambda i: (0, i))
    square = pl.BlockSpec((step, HD, HD), lambda i: (i, 0, 0))
    wide = jax.ShapeDtypeStruct((length, inner), BF16)
    full = jax.ShapeDtypeStruct((length, inner), F32)
    kernel = functools.partial(grads_kernel, 256)
    operands = [queries, keys, values, high, low, state]
    kernel, operands, in_specs = tied(
        kernel, operands, [rows, rows, rows, rows, rows, square], deps
    )
    return pl.pallas_call(
        kernel,
        grid=(heads // step,),
        in_specs=in_specs,
        out_specs=[rows, rows, rows],
        out_shape=[wide, full, full],
        compiler_params=params(),
        cost_estimate=cost(10 * length * length * inner, 20 * length * inner),
    )(*operands)


def later_kernel(k_ref, v_ref, dk_ref, dv_ref, l_ref, dk_out, dv_out):
    groups = HD // (2 * l_ref.shape[1])
    for head in range(l_ref.shape[0] // 2):
        cols = slice(head * HD, (head + 1) * HD)
        later = jnp.concatenate(
            [
                l_ref[2 * head + piece, :, group * HD : (group + 1) * HD]
                for piece in range(2)
                for group in range(groups)
            ],
            axis=0,
        )
        dk_out[:, cols] = (dk_ref[:, cols] + dot(v_ref[:, cols], later, NT)).astype(BF16)
        dv_out[:, cols] = (dv_ref[:, cols] + dot(k_ref[:, cols], later, NN)).astype(BF16)


def later_grads(keys, values, key_part, value_part, parts, deps):
    length, inner = keys.shape
    heads = inner // HD
    step = 4
    rows = pl.BlockSpec((length, step * HD), lambda i: (0, i))
    wide = jax.ShapeDtypeStruct((length, inner), BF16)
    last = parts.shape[1] // 16 - 1
    in_specs = [
        rows,
        rows,
        rows,
        rows,
        pl.BlockSpec((2 * step, 16, parts.shape[2]), lambda i: (i, last, 0)),
    ]
    operands = [keys, values, key_part, value_part, parts]
    kernel, operands, in_specs = tied(later_kernel, operands, in_specs, deps)
    return pl.pallas_call(
        kernel,
        grid=(heads // step,),
        in_specs=in_specs,
        out_specs=[rows, rows],
        out_shape=[wide, wide],
        compiler_params=params(),
        cost_estimate=cost(4 * length * HD * inner, 16 * length * inner),
    )(*operands)


def mixed_kernel(sel_ref, *refs):
    blocks, w_ref, o_ref = refs[:-2], refs[-2], refs[-1]
    half = HD // 2
    total = None
    for place, block in enumerate(blocks):
        rows = []
        for head in range(block.shape[1] // half):
            first = sel_ref[2 * place] * 1024 + sel_ref[2 * place + 1] * half + head * HD
            rows.append(w_ref[pl.ds(pl.multiple_of(first, half), half), :])
        term = dot(block[...], jnp.concatenate(rows, axis=0), NN)
        total = term if total is None else total + term
    o_ref[...] = total.astype(BF16)


def mix(sel, blocks, w_out, deps):
    length, width = blocks[0].shape
    inner, features = w_out.shape
    tile = 256
    whole = pl.BlockSpec((length, width), lambda j, s: (0, 0))
    in_specs = [whole] * len(blocks) + [pl.BlockSpec((inner, tile), lambda j, s: (0, j))]
    kernel, operands, in_specs = tied(mixed_kernel, [sel, *blocks, w_out], in_specs, deps)
    return pl.pallas_call(
        kernel,
        grid_spec=pltpu.PrefetchScalarGridSpec(
            num_scalar_prefetch=1,
            grid=(features // tile,),
            in_specs=in_specs,
            out_specs=pl.BlockSpec((length, tile), lambda j, s: (0, j)),
        ),
        out_shape=jax.ShapeDtypeStruct((length, features), BF16),
        compiler_params=params(),
        cost_estimate=cost(2 * length * inner * features, 2 * inner * features),
    )(*operands)


def weight_kernel(sel_ref, a0_ref, a1_ref, b0_ref, b1_ref, m0_ref, m1_ref, *rest):
    o_ref = rest[-1]
    count, size = o_ref.shape[:2]
    for source, (first, second) in enumerate(((a0_ref, a1_ref), (b0_ref, b1_ref))):

        @pl.when(pl.program_id(0) == source)
        def _(first=first, second=second):
            total = dot(first[...], m0_ref[...], TN) + dot(second[...], m1_ref[...], TN)
            for piece in range(count):
                o_ref[piece] = total[piece * size : (piece + 1) * size].astype(BF16)


def weight_grad(sel, mine, other, grads, across, index, target=None, deps=()):
    length, width = mine[0].shape
    features = grads[0].shape[1]
    size = 2 * width // across
    tile = 512
    tiles, count = width // tile, tile // size
    last = tiles - 1

    def place(i, j, s):
        return ((s[0] + i - 2 * s[0] * i) * tiles + j, index, 0)

    first_rows = pl.BlockSpec((length, tile), lambda i, j, s: (0, jnp.where(i == 0, j, last)))
    second_rows = pl.BlockSpec((length, tile), lambda i, j, s: (0, jnp.where(i == 0, 0, j)))
    whole = pl.BlockSpec((length, features), lambda i, j, s: (0, 0))
    in_specs = [first_rows, first_rows, second_rows, second_rows, whole, whole]
    operands = [sel, mine[0], mine[1], other[0], other[1], *grads]
    aliases = {}
    if target is not None:
        in_specs.append(pl.BlockSpec(memory_space=pl.ANY))
        operands.append(target)
        aliases = {len(operands) - 1: 0}
    kernel, operands, in_specs = tied(weight_kernel, operands, in_specs, deps)
    return pl.pallas_call(
        kernel,
        grid_spec=pltpu.PrefetchScalarGridSpec(
            num_scalar_prefetch=1,
            grid=(2, tiles),
            in_specs=in_specs,
            out_specs=pl.BlockSpec((count, size, features), place),
        ),
        out_shape=jax.ShapeDtypeStruct((across, 2 * size + 16, features), BF16),
        input_output_aliases=aliases,
        compiler_params=params(),
        cost_estimate=cost(8 * length * width * features, 4 * width * features),
    )(*operands)


def per_device(query_rows, key_rows, value_rows, gate_input, norm_gain, w_out, mixed_grad):
    length, inner_dev = query_rows.shape
    heads_dev = inner_dev // HD
    features = w_out.shape[1]
    planes, across = 2, 16
    ctx, fsdp = lax.axis_index("ctx"), lax.axis_index("fsdp")
    y_lo = ctx // across
    y_hi, core = fsdp // 2, fsdp % 2
    groups = [[y * across + i for i in range(across)] for y in range(planes)]
    core_swap = [(0, 1), (1, 0), (2, 3), (3, 2)]
    hi_swap = [(0, 2), (1, 3), (2, 0), (3, 1)]
    lo_swap = [(i, (i + across) % (2 * across)) for i in range(2 * across)]

    def swap_core(array):
        return lax.ppermute(array, "fsdp", core_swap)

    def swap_hi(array):
        return lax.ppermute(array, "fsdp", hi_swap)

    def swap_lo(array):
        return lax.ppermute(array, "ctx", lo_swap)

    def exchange(array):
        return lax.all_to_all(array, "ctx", 0, 0, axis_index_groups=groups)

    def sums_before(pieces, offset, reverse, target=None, deps=()):
        use = (y_lo == (0 if reverse else 1)).astype(jnp.int32).reshape(1)
        return running_sum(pieces, offset, use, reverse, target, deps)

    def split_states(local):
        return exchange(local.reshape(across, heads_dev * HD // across, HD))

    gain = norm_gain.reshape(1, inner_dev)
    peer, far = fsdp + 1 - 2 * core, (fsdp + 2) % 4
    far_peer = (peer + 2) % 4

    def term(place, dtype, received=None, deps=()):
        return head_term(place, mixed_grad, w_out, inner_dev, dtype, received, deps)

    def term(places, dtype, received=None, part=0):
        return head_term(places, mixed_grad, w_out, inner_dev, dtype, received, part)

    grad_pair = swap_lo(mixed_grad)
    sent = term([far_peer, peer], BF16)
    got = swap_core(sent)
    local_state = block_states(after(key_rows, sent), value_rows)
    pieces = split_states(local_state)
    far_part = term([far], BF16, got, 0)[0]
    total = jnp.sum(after(pieces, far_part), axis=0)
    offset = swap_lo(total)
    grad_far = swap_hi(after(far_part, offset, grad_pair))
    sums = sums_before(after(pieces, far_part), offset, False)
    grad_own = term([after(fsdp, sums)], F32, got, 1)[0]
    prev_state = exchange(sums).reshape(heads_dev, HD, HD)

    half = y_lo.astype(jnp.int32).reshape(1)
    out, out_other, attn = head_outputs(
        half, after(query_rows, grad_own), key_rows, value_rows, gate_input, gain, prev_state, []
    )
    gate_grad, high, low, grad_state = head_back(
        query_rows, gate_input, gain, attn, grad_own, grad_far
    )
    later_pieces = split_states(grad_state)
    later_total = jnp.sum(later_pieces, axis=0)

    across_y = []
    for place in range(2 * across):
        for part in range(4):
            target = ((place + across) % (2 * across)) * 4 + (part + 2) % 4
            across_y.append((place * 4 + part, target))
    out_pair = swap_lo(out_other)
    out_far = swap_hi(out)
    out_far_pair = lax.ppermute(out_other, ("ctx", "fsdp"), across_y)
    out_core, out_pair_core = (
        swap_core(after(out, grad_state)), swap_core(after(out_pair, grad_state))
    )
    out_far_core, out_far_pair_core = swap_core(out_far), swap_core(out_far_pair)
    select = core.astype(jnp.int32).reshape(1)
    grads = [mixed_grad, grad_pair]
    weight = weight_grad(
        select, [out, out_pair], [out_core, out_pair_core], grads, across, 0, deps=[grad_state]
    )
    weight = weight_grad(
        select, [out_far, out_far_pair], [out_far_core, out_far_pair_core], grads, across, 1,
        weight,
    )
    later_offset = swap_lo(later_total)
    weight = sums_before(later_pieces, later_offset, True, weight)
    parts = exchange(weight)
    far_other = swap_hi(out_other)
    query_grad, key_part, value_part = head_grads(
        query_rows, key_rows, value_rows, high, low, prev_state, [weight]
    )

    blocks = [out, out_other, out_core, swap_core(out_other)]
    blocks += [out_far, far_other, out_far_core, swap_core(far_other)]
    order = []
    for heads in (fsdp, peer, far, far_peer):
        order += [heads, y_lo, heads, 1 - y_lo]
    order = jnp.stack(order).astype(jnp.int32)
    mixed = mix(order, blocks, w_out, [query_grad])

    parts = after(parts, mixed)
    key_grad, value_grad = later_grads(key_rows, value_rows, key_part, value_part, parts, [])
    size = 2 * inner_dev // (2 * across)
    near_sum = jnp.sum(parts[:, :size].astype(F32), axis=0)
    far_sum = jnp.sum(parts[:, size : 2 * size].astype(F32), axis=0)
    keeps = y_hi == y_lo
    kept = jnp.where(keeps, near_sum, far_sum)
    received = swap_lo(jnp.where(keeps, far_sum, near_sum))
    w_out_grad = jnp.where(
        y_lo == 0,
        jnp.concatenate([kept, received], axis=0),
        jnp.concatenate([received, kept], axis=0),
    )
    return (mixed, w_out_grad, query_grad, key_grad, value_grad, gate_grad)


def solution(mesh):
    return jax.shard_map(
        per_device,
        mesh=mesh,
        in_specs=(
            P("ctx", "fsdp"),
            P("ctx", "fsdp"),
            P("ctx", "fsdp"),
            P("ctx", "fsdp"),
            P("fsdp"),
            P(None, "fsdp"),
            P("ctx", "fsdp"),
        ),
        out_specs=(
            P("ctx", "fsdp"),
            P("ctx", "fsdp"),
            P("ctx", "fsdp"),
            P("ctx", "fsdp"),
            P("ctx", "fsdp"),
            P("ctx", "fsdp"),
        ),
        check_vma=False,
    )
```

```python
import functools

import jax
import jax.numpy as jnp
from jax import lax
from jax.experimental import pallas as pl
from jax.experimental.pallas import tpu as pltpu
from jax.sharding import PartitionSpec as P

HD = 128
F32 = jnp.float32
BF16 = jnp.bfloat16
VMEM_LIMIT = 44 * 1024 * 1024

NT = (((1,), (1,)), ((), ()))
TN = (((0,), (0,)), ((), ()))
NN = (((1,), (0,)), ((), ()))


def dot(a, b, dims):
    return lax.dot_general(a, b, dims, preferred_element_type=F32)


def after(array, *others):
    return lax.optimization_barrier((array,) + others)[0]


def tied(kernel, operands, in_specs, deps):
    count = len(operands)

    def run(*refs):
        kernel(*refs[:count], *refs[count + len(deps) :])

    specs = [pl.BlockSpec(memory_space=pl.ANY)] * len(deps)
    return run, list(operands) + list(deps), list(in_specs) + specs


def params():
    return pltpu.CompilerParams(vmem_limit_bytes=VMEM_LIMIT)


def cost(flops, nbytes):
    return pl.CostEstimate(flops=flops, bytes_accessed=nbytes, transcendentals=0)


def state_kernel(k_ref, v_ref, s_ref):
    for head in range(s_ref.shape[0]):
        cols = slice(head * HD, (head + 1) * HD)
        s_ref[head] = dot(k_ref[:, cols], v_ref[:, cols], TN)


def block_states(keys, values):
    length, inner = keys.shape
    heads = inner // HD
    step = 4
    rows = pl.BlockSpec((length, step * HD), lambda i: (0, i))
    return pl.pallas_call(
        state_kernel,
        grid=(heads // step,),
        in_specs=[rows, rows],
        out_specs=pl.BlockSpec((step, HD, HD), lambda i: (i, 0, 0)),
        out_shape=jax.ShapeDtypeStruct((heads, HD, HD), F32),
        compiler_params=params(),
        cost_estimate=cost(2 * length * inner * HD, 4 * length * inner),
    )(keys, values)


def running_kernel(reverse, count, use_ref, p_ref, offset_ref, *rest):
    out_ref = rest[-1]
    rows, lanes = out_ref.shape[1], p_ref.shape[2]
    groups = p_ref.shape[1] // rows
    if out_ref.shape[2] > groups * lanes:
        out_ref[...] = jnp.zeros(out_ref.shape, out_ref.dtype)
    total = offset_ref[...] * use_ref[0].astype(F32)
    for step in range(count):
        place = count - 1 - step if reverse else step
        piece = total.astype(out_ref.dtype)
        for group in range(groups):
            cols = slice(group * lanes, (group + 1) * lanes)
            out_ref[place, :, cols] = piece[group * rows : (group + 1) * rows]
        if step < count - 1:
            total = total + p_ref[place]


def running_sum(pieces, offset, use, reverse, target=None, deps=()):
    count, rows, lanes = pieces.shape
    in_specs = [
        pl.BlockSpec(memory_space=pltpu.SMEM),
        pl.BlockSpec(pieces.shape, lambda i: (0, 0, 0)),
        pl.BlockSpec(offset.shape, lambda i: (0, 0)),
    ]
    operands = [use, pieces, offset]
    if target is None:
        aliases = {}
        out_spec = pl.BlockSpec(pieces.shape, lambda i: (0, 0, 0))
        out_shape = jax.ShapeDtypeStruct(pieces.shape, BF16)
    else:
        aliases = {3: 0}
        in_specs.append(pl.BlockSpec(memory_space=pl.ANY))
        operands.append(target)
        last = target.shape[1] // 16 - 1
        out_spec = pl.BlockSpec((count, 16, target.shape[2]), lambda i: (0, last, 0))
        out_shape = jax.ShapeDtypeStruct(target.shape, BF16)
    kernel = functools.partial(running_kernel, reverse, count)
    kernel, operands, in_specs = tied(kernel, operands, in_specs, deps)
    return pl.pallas_call(
        kernel,
        grid=(1,),
        in_specs=in_specs,
        out_specs=out_spec,
        out_shape=out_shape,
        input_output_aliases=aliases,
        compiler_params=params(),
        cost_estimate=cost(count * rows * lanes, 6 * count * rows * lanes),
    )(*operands)


def head_term_kernel(sel_ref, a_ref, w_ref, o_ref):
    o_ref[0] = dot(a_ref[...], w_ref[...], NT).astype(o_ref.dtype)


def head_sum_kernel(sel_ref, a_ref, w_ref, r_ref, o_ref):
    total = dot(a_ref[...], w_ref[...], NT) + r_ref[0].astype(F32)
    o_ref[0] = total.astype(o_ref.dtype)


def head_term(places, grad, w_out, width, dtype, received=None, part=0):
    length, features = grad.shape
    count = len(places)
    tile = 512 if count == 1 else width
    tiles = width // tile
    in_specs = [
        pl.BlockSpec((length, features), lambda i, j, s: (0, 0)),
        pl.BlockSpec((tile, features), lambda i, j, s: (s[i] * tiles + j, 0)),
    ]
    operands = [jnp.stack(places).astype(jnp.int32), grad, w_out]
    if received is not None:
        in_specs.append(pl.BlockSpec((1, length, tile), lambda i, j, s: (part, 0, j)))
        operands.append(received)
    return pl.pallas_call(
        head_term_kernel if received is None else head_sum_kernel,
        grid_spec=pltpu.PrefetchScalarGridSpec(
            num_scalar_prefetch=1,
            grid=(count, tiles),
            in_specs=in_specs,
            out_specs=pl.BlockSpec((1, length, tile), lambda i, j, s: (i, 0, j)),
        ),
        out_shape=jax.ShapeDtypeStruct((count, length, width), dtype),
        compiler_params=params(),
        cost_estimate=cost(2 * length * features * width, 4 * width * features),
    )(*operands)


def score_rows(q_ref, k_ref, first, size):
    last = first + size
    scores = dot(q_ref[first:last], k_ref[:last], NT)
    return masked(scores, first)


def masked(scores, first):
    size = scores.shape[0]
    rows = lax.broadcasted_iota(jnp.int32, (size, size), 0)
    cols = lax.broadcasted_iota(jnp.int32, (size, size), 1)
    last = jnp.where(cols <= rows, scores[:, first:], 0.0).astype(BF16)
    if not first:
        return last
    return jnp.concatenate([scores[:, :first].astype(BF16), last], axis=1)


def sigmoid(gate):
    return 0.5 * jnp.tanh(0.5 * gate.astype(F32)) + 0.5


def head_out_kernel(
    part, half_ref, q_ref, k_ref, v_ref, g_ref, gain_ref, s_ref, mine_ref, other_ref, attn_ref
):
    length = q_ref.shape[0]
    half = HD // 2
    lane = lax.broadcasted_iota(jnp.int32, (part, HD), 1)
    upper = half_ref[0] == 1
    for pair in range(s_ref.shape[0] // 2):
        packed = slice(pair * HD, (pair + 1) * HD)
        for first in range(0, length, part):
            last = first + part
            outs = []
            for head in (2 * pair, 2 * pair + 1):
                cols = slice(head * HD, (head + 1) * HD)
                queries = q_ref[first:last, cols]
                scores = masked(dot(queries, k_ref[:last, cols], NT), first)
                attn = dot(scores, v_ref[:last, cols], NN) + dot(queries, s_ref[head], NN)
                inv = lax.rsqrt(jnp.mean(attn * attn, axis=-1, keepdims=True) + 1e-06)
                outs.append(attn * inv * gain_ref[:, cols] * sigmoid(g_ref[first:last, cols]))
                attn_ref[first:last, cols] = attn
            low = jnp.where(lane < half, outs[0], pltpu.roll(outs[1], half, 1))
            high = jnp.where(lane < half, pltpu.roll(outs[0], half, 1), outs[1])
            mine_ref[first:last, packed] = jnp.where(upper, high, low).astype(BF16)
            other_ref[first:last, packed] = jnp.where(upper, low, high).astype(BF16)


def head_outputs(half, queries, keys, values, gate, gain, state, deps):
    length, inner = queries.shape
    heads = inner // HD
    step = 4
    rows = pl.BlockSpec((length, step * HD), lambda i: (0, i))
    packed_rows = pl.BlockSpec((length, step * HD // 2), lambda i: (0, i))
    square = pl.BlockSpec((step, HD, HD), lambda i: (i, 0, 0))
    packed = jax.ShapeDtypeStruct((length, inner // 2), BF16)
    in_specs = [
        pl.BlockSpec(memory_space=pltpu.SMEM),
        rows,
        rows,
        rows,
        rows,
        pl.BlockSpec((1, step * HD), lambda i: (0, i)),
        square,
    ]
    operands = [half, queries, keys, values, gate, gain, state]
    kernel = functools.partial(head_out_kernel, 256)
    kernel, operands, in_specs = tied(kernel, operands, in_specs, deps)
    return pl.pallas_call(
        kernel,
        grid=(heads // step,),
        in_specs=in_specs,
        out_specs=[packed_rows, packed_rows, rows],
        out_shape=[packed, packed, jax.ShapeDtypeStruct((length, inner), F32)],
        compiler_params=params(),
        cost_estimate=cost(4 * length * length * inner, 14 * length * inner),
    )(*operands)


def head_back_kernel(
    q_ref, g_ref, gain_ref, attn_ref, own_ref, far_ref, gate_ref, hi_ref, lo_ref, state_ref
):
    for head in range(state_ref.shape[0]):
        cols = slice(head * HD, (head + 1) * HD)
        gain = gain_ref[:, cols]
        attn = attn_ref[:, cols]
        inv = lax.rsqrt(jnp.mean(attn * attn, axis=-1, keepdims=True) + 1e-06)
        sig = sigmoid(g_ref[:, cols])
        grad = own_ref[:, cols] + far_ref[:, cols].astype(F32)
        unit = attn * inv
        scaled = grad * sig * gain
        product = scaled * unit
        gate_ref[:, cols] = (product * (1.0 - sig)).astype(BF16)
        full = inv * (scaled - unit * jnp.mean(product, axis=-1, keepdims=True))
        high = full.astype(BF16)
        hi_ref[:, cols] = high
        lo_ref[:, cols] = (full - high.astype(F32)).astype(BF16)
        state_ref[head] = dot(q_ref[:, cols], high, TN)


def head_back(queries, gate, gain, attn, own, far):
    length, inner = queries.shape
    heads = inner // HD
    step = 4
    rows = pl.BlockSpec((length, step * HD), lambda i: (0, i))
    square = pl.BlockSpec((step, HD, HD), lambda i: (i, 0, 0))
    wide = jax.ShapeDtypeStruct((length, inner), BF16)
    return pl.pallas_call(
        head_back_kernel,
        grid=(heads // step,),
        in_specs=[rows, rows, pl.BlockSpec((1, step * HD), lambda i: (0, i)), rows, rows, rows],
        out_specs=[rows, rows, rows, square],
        out_shape=[wide, wide, wide, jax.ShapeDtypeStruct((heads, HD, HD), F32)],
        compiler_params=params(),
        cost_estimate=cost(2 * length * HD * inner, 20 * length * inner),
    )(queries, gate, gain, attn, own, far)


def grads_kernel(
    part, q_ref, k_ref, v_ref, hi_ref, lo_ref, s_ref, dq_ref, dk_ref, dv_ref
):
    length = q_ref.shape[0]
    for head in range(s_ref.shape[0]):
        cols = slice(head * HD, (head + 1) * HD)
        for first in range(0, length, part):
            last = first + part
            queries, high = q_ref[first:last, cols], hi_ref[first:last, cols]
            keys, values = k_ref[:last, cols], v_ref[:last, cols]
            scores = masked(dot(queries, keys, NT), first)
            prob = dot(high, values, NT) + dot(lo_ref[first:last, cols], values, NT)
            prob = masked(prob, first)
            dq = dot(prob, keys, NN) + dot(high, s_ref[head], NT)
            dq_ref[first:last, cols] = dq.astype(BF16)
            dk = dot(prob, queries, TN)
            dv = dot(scores, high, TN)
            if first:
                dk_ref[:first, cols] += dk[:first]
                dv_ref[:first, cols] += dv[:first]
            dk_ref[first:last, cols] = dk[first:]
            dv_ref[first:last, cols] = dv[first:]


def head_grads(queries, keys, values, high, low, state, deps):
    length, inner = queries.shape
    heads = inner // HD
    step = 2
    rows = pl.BlockSpec((length, step * HD), lambda i: (0, i))
    square = pl.BlockSpec((step, HD, HD), lambda i: (i, 0, 0))
    wide = jax.ShapeDtypeStruct((length, inner), BF16)
    full = jax.ShapeDtypeStruct((length, inner), F32)
    kernel = functools.partial(grads_kernel, 256)
    operands = [queries, keys, values, high, low, state]
    kernel, operands, in_specs = tied(
        kernel, operands, [rows, rows, rows, rows, rows, square], deps
    )
    return pl.pallas_call(
        kernel,
        grid=(heads // step,),
        in_specs=in_specs,
        out_specs=[rows, rows, rows],
        out_shape=[wide, full, full],
        compiler_params=params(),
        cost_estimate=cost(10 * length * length * inner, 20 * length * inner),
    )(*operands)


def later_kernel(k_ref, v_ref, dk_ref, dv_ref, l_ref, dk_out, dv_out):
    groups = HD // (2 * l_ref.shape[1])
    for head in range(l_ref.shape[0] // 2):
        cols = slice(head * HD, (head + 1) * HD)
        later = jnp.concatenate(
            [
                l_ref[2 * head + piece, :, group * HD : (group + 1) * HD]
                for piece in range(2)
                for group in range(groups)
            ],
            axis=0,
        )
        dk_out[:, cols] = (dk_ref[:, cols] + dot(v_ref[:, cols], later, NT)).astype(BF16)
        dv_out[:, cols] = (dv_ref[:, cols] + dot(k_ref[:, cols], later, NN)).astype(BF16)


def later_grads(keys, values, key_part, value_part, parts, deps):
    length, inner = keys.shape
    heads = inner // HD
    step = 4
    rows = pl.BlockSpec((length, step * HD), lambda i: (0, i))
    wide = jax.ShapeDtypeStruct((length, inner), BF16)
    last = parts.shape[1] // 16 - 1
    in_specs = [
        rows,
        rows,
        rows,
        rows,
        pl.BlockSpec((2 * step, 16, parts.shape[2]), lambda i: (i, last, 0)),
    ]
    operands = [keys, values, key_part, value_part, parts]
    kernel, operands, in_specs = tied(later_kernel, operands, in_specs, deps)
    return pl.pallas_call(
        kernel,
        grid=(heads // step,),
        in_specs=in_specs,
        out_specs=[rows, rows],
        out_shape=[wide, wide],
        compiler_params=params(),
        cost_estimate=cost(4 * length * HD * inner, 16 * length * inner),
    )(*operands)


def mixed_kernel(sel_ref, *refs):
    blocks, w_ref, o_ref = refs[:-2], refs[-2], refs[-1]
    half = HD // 2
    total = None
    for place, block in enumerate(blocks):
        rows = []
        for head in range(block.shape[1] // half):
            first = sel_ref[2 * place] * 1024 + sel_ref[2 * place + 1] * half + head * HD
            rows.append(w_ref[pl.ds(pl.multiple_of(first, half), half), :])
        term = dot(block[...], jnp.concatenate(rows, axis=0), NN)
        total = term if total is None else total + term
    o_ref[...] = total.astype(BF16)


def mix(sel, blocks, w_out, deps):
    length, width = blocks[0].shape
    inner, features = w_out.shape
    tile = 256
    whole = pl.BlockSpec((length, width), lambda j, s: (0, 0))
    in_specs = [whole] * len(blocks) + [pl.BlockSpec((inner, tile), lambda j, s: (0, j))]
    kernel, operands, in_specs = tied(mixed_kernel, [sel, *blocks, w_out], in_specs, deps)
    return pl.pallas_call(
        kernel,
        grid_spec=pltpu.PrefetchScalarGridSpec(
            num_scalar_prefetch=1,
            grid=(features // tile,),
            in_specs=in_specs,
            out_specs=pl.BlockSpec((length, tile), lambda j, s: (0, j)),
        ),
        out_shape=jax.ShapeDtypeStruct((length, features), BF16),
        compiler_params=params(),
        cost_estimate=cost(2 * length * inner * features, 2 * inner * features),
    )(*operands)


def weight_kernel(sel_ref, a0_ref, a1_ref, b0_ref, b1_ref, m0_ref, m1_ref, *rest):
    o_ref = rest[-1]
    count, size = o_ref.shape[:2]
    for source, (first, second) in enumerate(((a0_ref, a1_ref), (b0_ref, b1_ref))):

        @pl.when(pl.program_id(0) == source)
        def _(first=first, second=second):
            total = dot(first[...], m0_ref[...], TN) + dot(second[...], m1_ref[...], TN)
            for piece in range(count):
                o_ref[piece] = total[piece * size : (piece + 1) * size].astype(BF16)


def weight_grad(sel, mine, other, grads, across, index, target=None, deps=()):
    length, width = mine[0].shape
    features = grads[0].shape[1]
    size = 2 * width // across
    tile = 512
    tiles, count = width // tile, tile // size
    last = tiles - 1

    def place(i, j, s):
        return ((s[0] + i - 2 * s[0] * i) * tiles + j, index, 0)

    first_rows = pl.BlockSpec((length, tile), lambda i, j, s: (0, jnp.where(i == 0, j, last)))
    second_rows = pl.BlockSpec((length, tile), lambda i, j, s: (0, jnp.where(i == 0, 0, j)))
    whole = pl.BlockSpec((length, features), lambda i, j, s: (0, 0))
    in_specs = [first_rows, first_rows, second_rows, second_rows, whole, whole]
    operands = [sel, mine[0], mine[1], other[0], other[1], *grads]
    aliases = {}
    if target is not None:
        in_specs.append(pl.BlockSpec(memory_space=pl.ANY))
        operands.append(target)
        aliases = {len(operands) - 1: 0}
    kernel, operands, in_specs = tied(weight_kernel, operands, in_specs, deps)
    return pl.pallas_call(
        kernel,
        grid_spec=pltpu.PrefetchScalarGridSpec(
            num_scalar_prefetch=1,
            grid=(2, tiles),
            in_specs=in_specs,
            out_specs=pl.BlockSpec((count, size, features), place),
        ),
        out_shape=jax.ShapeDtypeStruct((across, 2 * size + 16, features), BF16),
        input_output_aliases=aliases,
        compiler_params=params(),
        cost_estimate=cost(8 * length * width * features, 4 * width * features),
    )(*operands)


def per_device(query_rows, key_rows, value_rows, gate_input, norm_gain, w_out, mixed_grad):
    length, inner_dev = query_rows.shape
    heads_dev = inner_dev // HD
    features = w_out.shape[1]
    planes, across = 2, 16
    ctx, fsdp = lax.axis_index("ctx"), lax.axis_index("fsdp")
    y_lo = ctx // across
    y_hi, core = fsdp // 2, fsdp % 2
    groups = [[y * across + i for i in range(across)] for y in range(planes)]
    core_swap = [(0, 1), (1, 0), (2, 3), (3, 2)]
    hi_swap = [(0, 2), (1, 3), (2, 0), (3, 1)]
    lo_swap = [(i, (i + across) % (2 * across)) for i in range(2 * across)]

    def swap_core(array):
        return lax.ppermute(array, "fsdp", core_swap)

    def swap_hi(array):
        return lax.ppermute(array, "fsdp", hi_swap)

    def swap_lo(array):
        return lax.ppermute(array, "ctx", lo_swap)

    def exchange(array):
        return lax.all_to_all(array, "ctx", 0, 0, axis_index_groups=groups)

    def sums_before(pieces, offset, reverse, target=None, deps=()):
        use = (y_lo == (0 if reverse else 1)).astype(jnp.int32).reshape(1)
        return running_sum(pieces, offset, use, reverse, target, deps)

    def split_states(local):
        return exchange(local.reshape(across, heads_dev * HD // across, HD))

    gain = norm_gain.reshape(1, inner_dev)
    peer, far = fsdp + 1 - 2 * core, (fsdp + 2) % 4
    far_peer = (peer + 2) % 4

    def term(place, dtype, received=None, deps=()):
        return head_term(place, mixed_grad, w_out, inner_dev, dtype, received, deps)

    def term(places, dtype, received=None, part=0):
        return head_term(places, mixed_grad, w_out, inner_dev, dtype, received, part)

    grad_pair = swap_lo(mixed_grad)
    sent = term([far_peer, peer], BF16)
    got = swap_core(sent)
    local_state = block_states(after(key_rows, sent), value_rows)
    pieces = split_states(local_state)
    far_part = term([far], BF16, got, 0)[0]
    total = jnp.sum(after(pieces, far_part), axis=0)
    offset = swap_lo(total)
    grad_far = swap_hi(after(far_part, offset, grad_pair))
    sums = sums_before(after(pieces, far_part), offset, False)
    grad_own = term([after(fsdp, sums)], F32, got, 1)[0]
    prev_state = exchange(sums).reshape(heads_dev, HD, HD)

    half = y_lo.astype(jnp.int32).reshape(1)
    out, out_other, attn = head_outputs(
        half, after(query_rows, grad_own), key_rows, value_rows, gate_input, gain, prev_state, []
    )
    gate_grad, high, low, grad_state = head_back(
        query_rows, gate_input, gain, attn, grad_own, grad_far
    )
    later_pieces = split_states(grad_state)
    later_total = jnp.sum(later_pieces, axis=0)

    across_y = []
    for place in range(2 * across):
        for part in range(4):
            target = ((place + across) % (2 * across)) * 4 + (part + 2) % 4
            across_y.append((place * 4 + part, target))
    out_pair = swap_lo(out_other)
    out_far = swap_hi(out)
    out_far_pair = lax.ppermute(out_other, ("ctx", "fsdp"), across_y)
    out_core, out_pair_core = (
        swap_core(after(out, grad_state)), swap_core(after(out_pair, grad_state))
    )
    out_far_core, out_far_pair_core = swap_core(out_far), swap_core(out_far_pair)
    select = core.astype(jnp.int32).reshape(1)
    grads = [mixed_grad, grad_pair]
    weight = weight_grad(
        select, [out, out_pair], [out_core, out_pair_core], grads, across, 0, deps=[grad_state]
    )
    weight = weight_grad(
        select, [out_far, out_far_pair], [out_far_core, out_far_pair_core], grads, across, 1,
        weight,
    )
    later_offset = swap_lo(later_total)
    weight = sums_before(later_pieces, later_offset, True, weight)
    parts = exchange(weight)
    far_other = swap_hi(out_other)
    query_grad, key_part, value_part = head_grads(
        query_rows, key_rows, value_rows, high, low, prev_state, [weight]
    )

    blocks = [out, out_other, out_core, swap_core(out_other)]
    blocks += [out_far, far_other, out_far_core, swap_core(far_other)]
    order = []
    for heads in (fsdp, peer, far, far_peer):
        order += [heads, y_lo, heads, 1 - y_lo]
    order = jnp.stack(order).astype(jnp.int32)
    mixed = mix(order, blocks, w_out, [query_grad])

    parts = after(parts, mixed)
    key_grad, value_grad = later_grads(key_rows, value_rows, key_part, value_part, parts, [])
    size = 2 * inner_dev // (2 * across)
    near_sum = jnp.sum(parts[:, :size].astype(F32), axis=0)
    far_sum = jnp.sum(parts[:, size : 2 * size].astype(F32), axis=0)
    keeps = y_hi == y_lo
    kept = jnp.where(keeps, near_sum, far_sum)
    received = swap_lo(jnp.where(keeps, far_sum, near_sum))
    w_out_grad = jnp.where(
        y_lo == 0,
        jnp.concatenate([kept, received], axis=0),
        jnp.concatenate([received, kept], axis=0),
    )
    return (mixed, w_out_grad, query_grad, key_grad, value_grad, gate_grad)


def solution(mesh):
    return jax.shard_map(
        per_device,
        mesh=mesh,
        in_specs=(
            P("ctx", "fsdp"),
            P("ctx", "fsdp"),
            P("ctx", "fsdp"),
            P("ctx", "fsdp"),
            P("fsdp"),
            P(None, "fsdp"),
            P("ctx", "fsdp"),
        ),
        out_specs=(
            P("ctx", "fsdp"),
            P("ctx", "fsdp"),
            P("ctx", "fsdp"),
            P("ctx", "fsdp"),
            P("ctx", "fsdp"),
            P("ctx", "fsdp"),
        ),
        check_vma=False,
    )
```
